512 devices in a mesh: blk: 128 (over y, x, z_lo), rep: 4 (over z_hi, core).
Axes of the slice: x: 4, y: 4, z: 16 (z_hi: 2, z_lo: 8; z = z_hi * 8 + z_lo), core: 2. Of those that a mesh axis runs over, the one named last changes fastest.
Arguments:
- jacobian: float32 [32768, 4096], P(('blk', 'rep')), may hold values from -0.09375 to 0.09375
- cell_weight: float32 [4096], replicated, may hold values from 0.4 to 2
- neighbors: int32 [6, 4096], replicated, may hold values from -1 to 4095, as said below
Outputs:
- band: float32 [7, 32768, 256], P(None, 'blk', 'rep')
The draws below stay inside these ranges and needn't reach their ends.
Inputs may be any that keep to these rules, and one draw needn't show every extreme that they name: neighbors lists the face neighbours of the cells of a 32 x 32 x 4 grid under a numbering of the cells; the relation is symmetric.
All inputs are finite; a program needn't handle non-finite values.
Results may differ from the reference program's by a relative error of at most 0.0001.
Values sent between devices are 32-bit elements; how exact they have to be, the bound alone decides.
A program may use at most 64 MiB of HBM per device.

```python
import math
import jax
import jax.numpy as jnp
from jax import lax

SIDE = 32
LAYERS = 4
CELLS = 4096
ROWS = 256
HALF = 3
BAND = 7
QUADS = 32768
N_BLK = 128


def draw_neighbors(key, part):
    perm = jax.random.permutation(key, CELLS).astype(jnp.int32)
    grid = jnp.arange(CELLS, dtype=jnp.int32).reshape(LAYERS, SIDE, SIDE)
    padded = jnp.pad(grid, 1, constant_values=-1)
    shifted = [padded[2:, 1:-1, 1:-1], padded[:-2, 1:-1, 1:-1], padded[1:-1, 2:, 1:-1], padded[1:-1, :-2, 1:-1], padded[1:-1, 1:-1, 2:], padded[1:-1, 1:-1, :-2]]
    rows = []
    for other in shifted:
        flat = other.reshape(CELLS)
        safe = jnp.maximum(flat, 0)
        label = jnp.where(flat >= 0, perm[safe], -1).astype(jnp.int32)
        table = jnp.zeros((CELLS,), jnp.int32).at[perm].set(label)
        rows.append(table)
    return jnp.stack(rows, 0)


def steps_of(rng, extent, shards, least, largest):
    factor_of, own = 1.0, jax.random.fold_in(rng, 6)
    for position, parts in shards:
        steps = jnp.exp(jax.random.uniform(jax.random.fold_in(own, position), (parts,), jnp.float32, least / len(shards), largest / len(shards)))
        factor_of = factor_of * jnp.repeat(steps, extent[position] // parts).reshape([-1 if axis == position else 1 for axis in range(len(extent))])
    return factor_of


def scatter_about(key, shape, deviation, most, cuts=(), held_as=jnp.bfloat16):
    entries = deviation * jax.random.normal(key, shape, jnp.float32)
    if cuts:
        entries = entries * steps_of(key, shape, cuts, -0.22, 0.18)
    return jnp.clip(entries, -most, most).astype(held_as)


def setup_inputs(seed: int = 0) -> dict:
    arg_keys = jax.random.split(jax.random.key(seed), 4)
    return {
        "jacobian": scatter_about(arg_keys[0], (QUADS, CELLS), CELLS ** -0.5, 0.09375, ((0, 512),), jnp.float32),
        "cell_weight": jnp.clip(jnp.exp(jax.random.uniform(arg_keys[1], (CELLS,), jnp.float32, math.log(0.4), math.log(2.0))), 0.4, 2.0),
        "neighbors": draw_neighbors(jax.random.fold_in(arg_keys[3], 71), 0),
    }


def reference(jacobian, cell_weight, neighbors):
    scaled = jacobian * cell_weight[None, :]
    total = scaled
    for direction in range(6):
        index = neighbors[direction]
        safe = jnp.maximum(index, 0).astype(jnp.int32)
        picked = jnp.take(scaled, safe, axis=1)
        present = (index >= 0).astype(jnp.float32)
        total = total + 0.15 * picked * present[None, :]
    smoothed = total * cell_weight[None, :]
    panels_s = smoothed.reshape(N_BLK, ROWS, CELLS)
    panels_j = jacobian.reshape(N_BLK, ROWS, CELLS)
    tiles = []
    for k in range(BAND):
        rolled = jnp.roll(panels_j, -(k - HALF), axis=0)
        tile = jnp.einsum("prc,pqc->prq", panels_s, rolled, precision=lax.Precision.HIGHEST)
        tiles.append(tile.reshape(N_BLK * ROWS, ROWS))
    return jnp.stack(tiles, 0)
```

```python
import math

import jax
import jax.numpy as jnp
import numpy as np
from jax import lax
from jax.experimental import pallas as pl
from jax.experimental.pallas import tpu as pltpu
from jax.sharding import PartitionSpec as P

F32, BF16 = jnp.float32, jnp.bfloat16
MESH = pl.DeviceIdType.MESH
SIDE = 32
NT = (((1,), (1,)), ((), ()))


def sine(y, n):
    return math.sqrt(2 / 33) * math.sin(math.pi * (y + 1) * (n + 1) / 33)


def lookup(table_ref, index):
    parts = []
    for g in range(4):
        idx = index[8 * g : 8 * g + 8]
        row, lane = idx >> 7, idx & 127
        out = jnp.zeros((8, 128), jnp.int32)
        for s in range(32):
            line = jnp.broadcast_to(table_ref[s : s + 1, :], (8, 128))
            got = jnp.take_along_axis(line, lane, axis=1, mode="promise_in_bounds")
            out = jnp.where(row == s, got, out)
        parts.append(out)
    return jnp.concatenate(parts, 0)


def steps_to_end(near, rounds, table_ref, own):
    value = jnp.where(near >= 0, near + 4096, own)
    for _ in range(rounds):
        table_ref[...] = value
        index = value & 4095
        value = (value - index) + lookup(table_ref, index)
    return value >> 12


def local_kernel(j_ref, w_ref, nb_ref, y_ref, table, first, second, hi, lo, onehot, acc):
    own = lax.broadcasted_iota(jnp.int32, (32, 128), 0) * 128 + lax.broadcasted_iota(jnp.int32, (32, 128), 1)
    missing = [jnp.where(nb_ref[d] < 0, 1.0, 0.0).astype(F32) for d in range(6)]
    count = [jnp.sum(m) for m in missing]

    def pick(flags, arrays):
        total = flags[0] * arrays[0]
        for flag, array in zip(flags[1:], arrays[1:]):
            total = total + flag * array
        return total

    def leading(conds):
        seen, flags = jnp.int32(0), []
        for cond in conds:
            flag = jnp.where(cond, 1, 0) * (1 - seen)
            seen = seen + flag
            flags.append(flag)
        return flags

    nbs = [nb_ref[d] for d in range(6)]
    deep = leading([c > 512.0 for c in count])
    one = leading([c < 512.0 for c in count])
    face = pick([f.astype(F32) for f in one], missing)
    meet = [jnp.sum(face * m) for m in missing]
    two = leading([(c < 512.0) & (m > 0.5) & (f == 0) for c, m, f in zip(count, meet, one)])
    ycoord = steps_to_end(pick(one, nbs), 5, table, own)
    xcoord = steps_to_end(pick(two, nbs), 5, table, own)
    layer = steps_to_end(pick(deep, nbs), 2, table, own)
    first[...] = ycoord >> 2
    second[...] = (ycoord & 3) * 128 + layer * 32 + xcoord

    for s in range(32):
        cols = slice(128 * s, 128 * s + 128)
        js = j_ref[:, cols] * w_ref[s : s + 1, :]
        top = js.astype(BF16)
        rest = (js - top.astype(F32)).astype(BF16)
        arow = jnp.broadcast_to(first[s : s + 1, :], (64, 128))
        for a in range(8):
            mask = jnp.where(arow == a, 1.0, 0.0).astype(BF16)
            hi[64 * a : 64 * a + 64, cols] = top * mask
            lo[64 * a : 64 * a + 64, cols] = rest * mask
        brow = jnp.broadcast_to(second[s : s + 1, :], (512, 128))
        onehot[:, cols] = jnp.where(brow == lax.broadcasted_iota(jnp.int32, (512, 128), 0), 1.0, 0.0).astype(BF16)

    for n in range(2):
        part = slice(256 * n, 256 * n + 256)
        acc[:, part] = lax.dot_general(hi[...], onehot[part, :], NT, preferred_element_type=F32) + lax.dot_general(
            lo[...], onehot[part, :], NT, preferred_element_type=F32
        )

    @pl.loop(0, 8)
    def _(g):
        rows = lambda a: pl.ds(pl.multiple_of(a * 64 + g * 8, 8), 8)
        z = lambda y: acc[rows(y // 4), 128 * (y % 4) : 128 * (y % 4) + 128]
        even, odd = [], []
        for y in range(16):
            p, q = z(y), z(31 - y)
            even.append(p + q)
            odd.append(p - q)
        for n in range(32):
            terms = odd if n % 2 else even
            total = terms[0] * sine(0, n)
            for y in range(1, 16):
                total = total + terms[y] * sine(y, n)
            y_ref[n // 2, pl.ds(pl.multiple_of(g * 8, 8), 8), 128 * (n % 2) : 128 * (n % 2) + 128] = total


def local_part(jacobian, cell_weight, neighbors):
    vmem = pl.BlockSpec(memory_space=pltpu.VMEM)
    return pl.pallas_call(
        local_kernel,
        out_shape=jax.ShapeDtypeStruct((16, 64, 256), F32),
        in_specs=[vmem] * 3,
        out_specs=vmem,
        scratch_shapes=[
            pltpu.VMEM((32, 128), jnp.int32),
            pltpu.VMEM((32, 128), jnp.int32),
            pltpu.VMEM((32, 128), jnp.int32),
            pltpu.VMEM((512, 4096), BF16),
            pltpu.VMEM((512, 4096), BF16),
            pltpu.VMEM((512, 4096), BF16),
            pltpu.VMEM((512, 512), F32),
        ],
        compiler_params=pltpu.CompilerParams(vmem_limit_bytes=40 * 2**20),
    )(jacobian, cell_weight.reshape(32, 128), neighbors.reshape(6, 32, 128))


def task_place(t, k8, e):
    col = t // 2
    half = (t + col) % 2
    return (half * 8 + k8) * 8 + col % 8, (col // 8) * 2 + e


def unless(cond, fn):
    pl.when(jnp.logical_not(cond))(fn)


def band_kernel(
    y_ref, lam_ref, adj_ref, o_ref,
    ra, rb, xhi, xlo, shi, slo, part, r1, r2, fin,
    sa_s, sa_r, sb_s, sb_r, sf_s, sf_r, s1_s, s1_r, s2_s, s2_r, so_s, so_r,
):
    B, R = lax.axis_index("blk"), lax.axis_index("rep")
    pln, zl, zh, e = B // 8, B % 8, R // 2, R % 2
    z = zh * 8 + zl
    half, k8 = pln // 8, pln % 8
    t = 2 * z + (half + zl) % 2

    def is_me(place):
        return (place[0] == B) & (place[1] == R)

    def send(src, dst, s_sem, r_sem, place):
        def there():
            pltpu.make_async_remote_copy(src, dst, s_sem, r_sem, device_id=place, device_id_type=MESH).start()

        def here():
            pltpu.make_async_copy(src, dst, r_sem).start()

        pl.when(is_me(place))(here)
        unless(is_me(place), there)

    def landed(ref, sem):
        pltpu.make_async_copy(ref, ref, sem).wait()

    def sent(ref, sem, place):
        unless(is_me(place), lambda: pltpu.make_async_copy(ref, ref, sem).wait())

    src_half = (zl // 4 + pln) % 2

    def a_to(k):
        return (src_half * 8 + k // 2) * 8 + zl, zh * 2 + k % 2

    def col_of(i):
        return 2 * i + (half + zl // 4) % 2

    def a_from(s):
        return col_of(s // 2) * 8 + zl, zh * 2 + s % 2

    def b_to(i):
        col = col_of(i)
        return pln * 8 + col % 8, (col // 8) * 2 + e

    def b_from(i):
        return pln * 8 + 4 * (t % 2) + i // 2, (i % 2) * 2 + e

    down = task_place((t + 31) % 32, k8, e)
    up = task_place((t + 1) % 32, k8, e)
    other = (B, zh * 2 + 1 - e)

    def mate(i):
        return (half * 8 + i) * 8 + zl, R

    panel = 4 * t + 2 * e + k8 // 4
    gap = k8 % 4

    def o_to(i):
        return (panel + (i // 4) * gap) % 128, i % 4

    def o_from(m):
        j = jnp.where(m < 3, 3 - m, m - 3)
        b = jnp.where(m < 3, (B - j + 128) % 128, B)
        q = 4 * (b % 4) + j
        return task_place(b // 4, q % 8, q // 8)

    barrier = pltpu.get_barrier_semaphore()

    def greet(place):
        unless(
            is_me(place),
            lambda: pl.semaphore_signal(barrier, inc=1, device_id=place, device_id_type=MESH),
        )

    greet(up)
    greet(other)
    pl.loop(0, 16)(lambda s: greet(a_from(s)))
    pl.loop(0, 8)(lambda s: greet(b_from(s)))
    pl.loop(0, 8)(lambda s: greet(mate(s)))
    pl.loop(0, 7)(lambda s: greet(o_from(s)))
    out_count = jnp.where(gap == 0, 4, 8)
    own_a = jnp.where(src_half == half, 1, 0)
    own_b = jnp.where((z + half + zl // 4) % 2 == 0, 1, 0)
    own_o = jnp.where((panel == B) | ((panel + gap) % 128 == B), 1, 0)
    pl.semaphore_wait(barrier, 2 + 16 + 8 + 7 + out_count - own_a - own_b - own_o)

    @pl.loop(0, 16)
    def _(n):
        k = (n + 2 * pln + 2) % 16
        slot = (pln // 2) * 2 + e
        send(y_ref.at[k], ra.at[slot], sa_s.at[k], sa_r.at[slot], a_to(k))

    @pl.loop(0, 16)
    def _(n):
        s = (n + pln + 2 * (z // 2)) % 16
        landed(ra.at[s], sa_r.at[s])
        slot = (zl % 4) * 4 + zh * 2 + s % 2
        send(ra.at[s], rb.at[slot], sb_s.at[s], sb_r.at[slot], b_to(s // 2))

    def split(p):
        rows = pl.ds(pl.multiple_of(p * 256, 256), 256)
        x = rb[pl.ds(p * 4, 4)].reshape(256, 256)
        top = x.astype(BF16)
        rest = (x - top.astype(F32)).astype(BF16)
        xhi[rows, :] = top
        xlo[rows, :] = rest
        return rows, x, top, rest

    @pl.loop(0, 4)
    def _(p):
        @pl.loop(0, 4)
        def _(i):
            landed(rb.at[p * 4 + i], sb_r.at[p * 4 + i])

        @pl.when(p < 3)
        def _():
            send(rb.at[pl.ds(p * 4, 4)], rb.at[pl.ds(16 + p * 4, 4)], sf_s.at[p], sf_r.at[p], down)

        rows, x, top, rest = split(p)
        beside = jnp.dot(top, adj_ref[...], preferred_element_type=F32)
        beside = beside + jnp.dot(rest, adj_ref[...], preferred_element_type=F32)
        smooth = x * lam_ref[pl.ds(2 * k8 + e, 1), :] + 0.15 * beside
        stop = smooth.astype(BF16)
        shi[rows, :] = stop
        slo[rows, :] = (smooth - stop.astype(F32)).astype(BF16)

    @pl.loop(0, 3)
    def _(p):
        landed(rb.at[pl.ds(16 + p * 4, 4)], sf_r.at[p])
        split(p + 4)

    def tile(q):
        p = pl.ds(pl.multiple_of((q // 4) * 256, 256), 256)
        o = pl.ds(pl.multiple_of((q // 4 + q % 4) * 256, 256), 256)
        total = lax.dot_general(shi[p, :], xlo[o, :], NT, preferred_element_type=F32)
        total = total + lax.dot_general(slo[p, :], xhi[o, :], NT, preferred_element_type=F32)
        return total + lax.dot_general(shi[p, :], xhi[o, :], NT, preferred_element_type=F32)

    @pl.loop(0, 8)
    def _(n):
        i = (k8 + 1 + n) % 8
        q = 8 * (1 - e) + i
        part[q] = tile(q)
        send(part.at[q], r1.at[i], s1_s.at[i], s1_r.at[i], other)

    @pl.loop(0, 8)
    def _(n):
        i = (k8 + 1 + n) % 8
        q = 8 * e + i
        total = tile(q)
        landed(r1.at[i], s1_r.at[i])
        part[q] = total + r1[i]

        @pl.when(n < 7)
        def _():
            send(part.at[q], r2.at[k8], s2_s.at[i], s2_r.at[k8], mate(i))

    r2[k8] = part[8 * e + k8]

    @pl.loop(0, 7)
    def _(n):
        i = (k8 + 7 - n) % 8
        landed(r2.at[i], s2_r.at[i])

    total = r2[0]
    for i in range(1, 8):
        total = total + r2[i]
    fin[pl.ds(0, 4)] = total.T.reshape(4, 64, 256)
    fin[pl.ds(4, 4)] = total.reshape(4, 64, 256)

    @pl.loop(0, out_count)
    def _(i):
        m = jnp.where(i < 4, 3 + gap, 3 - gap)
        send(fin.at[i], o_ref.at[m], so_s.at[i], so_r.at[m], o_to(i))

    pl.loop(0, 7)(lambda m: landed(o_ref.at[m], so_r.at[m]))

    pl.loop(0, 16)(lambda k: sent(y_ref.at[k], sa_s.at[k], a_to(k)))
    pl.loop(0, 16)(lambda s: sent(ra.at[s], sb_s.at[s], b_to(s // 2)))
    pl.loop(0, 3)(lambda p: sent(rb.at[pl.ds(p * 4, 4)], sf_s.at[p], down))
    pl.loop(0, 8)(lambda i: sent(part.at[8 * (1 - e) + i], s1_s.at[i], other))
    pl.loop(0, 8)(lambda i: sent(part.at[8 * e + i], s2_s.at[i], mate(i)))
    pl.loop(0, out_count)(lambda i: sent(fin.at[i], so_s.at[i], o_to(i)))


def band_part(spectral):
    lane = np.arange(128)
    x, layer = lane % 32, lane // 32
    near = np.abs(x[:, None] - x[None, :]) + np.abs(layer[:, None] - layer[None, :]) == 1
    adjacency = jnp.asarray(np.kron(np.eye(2), near), BF16)
    n = np.arange(32)
    lam = 1 + 0.15 * 2 * np.cos(np.pi * (n + 1) / 33)
    lam = jnp.asarray(np.repeat(lam, 128).reshape(16, 256), F32)
    vmem = pl.BlockSpec(memory_space=pltpu.VMEM)
    dma = pltpu.SemaphoreType.DMA
    counts = (16, 16, 16, 16, 3, 3, 8, 8, 8, 8, 8, 7)
    return pl.pallas_call(
        band_kernel,
        out_shape=jax.ShapeDtypeStruct((7, 64, 256), F32),
        in_specs=[vmem] * 3,
        out_specs=vmem,
        scratch_shapes=[
            pltpu.VMEM((16, 64, 256), F32),
            pltpu.VMEM((28, 64, 256), F32),
            pltpu.VMEM((1792, 256), BF16),
            pltpu.VMEM((1792, 256), BF16),
            pltpu.VMEM((1024, 256), BF16),
            pltpu.VMEM((1024, 256), BF16),
            pltpu.VMEM((16, 256, 256), F32),
            pltpu.VMEM((8, 256, 256), F32),
            pltpu.VMEM((8, 256, 256), F32),
            pltpu.VMEM((8, 64, 256), F32),
        ]
        + [dma((c,)) for c in counts],
        compiler_params=pltpu.CompilerParams(collective_id=0, has_side_effects=True, vmem_limit_bytes=40 * 2**20),
    )(spectral, lam, adjacency)


def per_device(jacobian, cell_weight, neighbors):
    spectral = local_part(jacobian, cell_weight, neighbors)
    return jnp.swapaxes(band_part(spectral), 1, 2)


def solution(mesh):
    return jax.shard_map(
        per_device,
        mesh=mesh,
        in_specs=(P(("blk", "rep"), None), P(), P()),
        out_specs=P(None, "blk", "rep"),
        check_vma=False,
    )
```

```python
import math

import jax
import jax.numpy as jnp
import numpy as np
from jax import lax
from jax.experimental import pallas as pl
from jax.experimental.pallas import tpu as pltpu
from jax.sharding import PartitionSpec as P

F32, BF16 = jnp.float32, jnp.bfloat16
MESH = pl.DeviceIdType.MESH
SIDE = 32
NT = (((1,), (1,)), ((), ()))


def sine(y, n):
    return math.sqrt(2 / 33) * math.sin(math.pi * (y + 1) * (n + 1) / 33)


def lookup(table_ref, index):
    parts = []
    for g in range(4):
        idx = index[8 * g : 8 * g + 8]
        row, lane = idx >> 7, idx & 127
        out = jnp.zeros((8, 128), jnp.int32)
        for s in range(32):
            line = jnp.broadcast_to(table_ref[s : s + 1, :], (8, 128))
            got = jnp.take_along_axis(line, lane, axis=1, mode="promise_in_bounds")
            out = jnp.where(row == s, got, out)
        parts.append(out)
    return jnp.concatenate(parts, 0)


def steps_to_end(near, rounds, table_ref, own):
    value = jnp.where(near >= 0, near + 4096, own)
    for _ in range(rounds):
        table_ref[...] = value
        index = value & 4095
        value = (value - index) + lookup(table_ref, index)
    return value >> 12


def local_kernel(j_ref, w_ref, nb_ref, y_ref, table, first, second, hi, lo, onehot, acc):
    own = lax.broadcasted_iota(jnp.int32, (32, 128), 0) * 128 + lax.broadcasted_iota(jnp.int32, (32, 128), 1)
    missing = [jnp.where(nb_ref[d] < 0, 1.0, 0.0).astype(F32) for d in range(6)]
    count = [jnp.sum(m) for m in missing]

    def pick(flags, arrays):
        total = flags[0] * arrays[0]
        for flag, array in zip(flags[1:], arrays[1:]):
            total = total + flag * array
        return total

    def leading(conds):
        seen, flags = jnp.int32(0), []
        for cond in conds:
            flag = jnp.where(cond, 1, 0) * (1 - seen)
            seen = seen + flag
            flags.append(flag)
        return flags

    nbs = [nb_ref[d] for d in range(6)]
    deep = leading([c > 512.0 for c in count])
    one = leading([c < 512.0 for c in count])
    face = pick([f.astype(F32) for f in one], missing)
    meet = [jnp.sum(face * m) for m in missing]
    two = leading([(c < 512.0) & (m > 0.5) & (f == 0) for c, m, f in zip(count, meet, one)])
    ycoord = steps_to_end(pick(one, nbs), 5, table, own)
    xcoord = steps_to_end(pick(two, nbs), 5, table, own)
    layer = steps_to_end(pick(deep, nbs), 2, table, own)
    first[...] = ycoord >> 2
    second[...] = (ycoord & 3) * 128 + layer * 32 + xcoord

    for s in range(32):
        cols = slice(128 * s, 128 * s + 128)
        js = j_ref[:, cols] * w_ref[s : s + 1, :]
        top = js.astype(BF16)
        rest = (js - top.astype(F32)).astype(BF16)
        arow = jnp.broadcast_to(first[s : s + 1, :], (64, 128))
        for a in range(8):
            mask = jnp.where(arow == a, 1.0, 0.0).astype(BF16)
            hi[64 * a : 64 * a + 64, cols] = top * mask
            lo[64 * a : 64 * a + 64, cols] = rest * mask
        brow = jnp.broadcast_to(second[s : s + 1, :], (512, 128))
        onehot[:, cols] = jnp.where(brow == lax.broadcasted_iota(jnp.int32, (512, 128), 0), 1.0, 0.0).astype(BF16)

    for n in range(2):
        part = slice(256 * n, 256 * n + 256)
        acc[:, part] = lax.dot_general(hi[...], onehot[part, :], NT, preferred_element_type=F32) + lax.dot_general(
            lo[...], onehot[part, :], NT, preferred_element_type=F32
        )

    @pl.loop(0, 8)
    def _(g):
        rows = lambda a: pl.ds(pl.multiple_of(a * 64 + g * 8, 8), 8)
        z = lambda y: acc[rows(y // 4), 128 * (y % 4) : 128 * (y % 4) + 128]
        even, odd = [], []
        for y in range(16):
            p, q = z(y), z(31 - y)
            even.append(p + q)
            odd.append(p - q)
        for n in range(32):
            terms = odd if n % 2 else even
            total = terms[0] * sine(0, n)
            for y in range(1, 16):
                total = total + terms[y] * sine(y, n)
            y_ref[n // 2, pl.ds(pl.multiple_of(g * 8, 8), 8), 128 * (n % 2) : 128 * (n % 2) + 128] = total


def local_part(jacobian, cell_weight, neighbors):
    vmem = pl.BlockSpec(memory_space=pltpu.VMEM)
    return pl.pallas_call(
        local_kernel,
        out_shape=jax.ShapeDtypeStruct((16, 64, 256), F32),
        in_specs=[vmem] * 3,
        out_specs=vmem,
        scratch_shapes=[
            pltpu.VMEM((32, 128), jnp.int32),
            pltpu.VMEM((32, 128), jnp.int32),
            pltpu.VMEM((32, 128), jnp.int32),
            pltpu.VMEM((512, 4096), BF16),
            pltpu.VMEM((512, 4096), BF16),
            pltpu.VMEM((512, 4096), BF16),
            pltpu.VMEM((512, 512), F32),
        ],
        compiler_params=pltpu.CompilerParams(vmem_limit_bytes=40 * 2**20),
    )(jacobian, cell_weight.reshape(32, 128), neighbors.reshape(6, 32, 128))


def task_place(t, k8, e):
    z = t % 16
    return ((t // 16) * 8 + k8) * 8 + z % 8, (z // 8) * 2 + e


def unless(cond, fn):
    pl.when(jnp.logical_not(cond))(fn)


def band_kernel(
    y_ref, lam_ref, adj_ref, o_ref,
    ra, rb, xhi, xlo, shi, slo, part, r1, r2, across, along,
    sa_s, sa_r, sb_s, sb_r, sf_s, sf_r, s1_s, s1_r, s2_s, s2_r, sx_s, sy_s, so_r,
):
    B, R = lax.axis_index("blk"), lax.axis_index("rep")
    pln, zl, zh, e = B // 8, B % 8, R // 2, R % 2
    z = zh * 8 + zl
    half, k8 = pln // 8, pln % 8
    t = half * 16 + z

    def is_me(place):
        return (place[0] == B) & (place[1] == R)

    def send(src, dst, s_sem, r_sem, place):
        def there():
            pltpu.make_async_remote_copy(src, dst, s_sem, r_sem, device_id=place, device_id_type=MESH).start()

        def here():
            pltpu.make_async_copy(src, dst, r_sem).start()

        pl.when(is_me(place))(here)
        unless(is_me(place), there)

    def landed(ref, sem):
        pltpu.make_async_copy(ref, ref, sem).wait()

    def sent(ref, sem, place):
        unless(is_me(place), lambda: pltpu.make_async_copy(ref, ref, sem).wait())

    def a_to(k):
        return (half * 8 + k // 2) * 8 + zl, zh * 2 + k % 2

    def b_to(i):
        there = 2 * i + zl // 4
        return pln * 8 + there % 8, (there // 8) * 2 + e

    def b_from(i):
        return pln * 8 + 4 * (z % 2) + i // 2, (i % 2) * 2 + e

    down = task_place((t + 31) % 32, k8, e)
    up = task_place((t + 1) % 32, k8, e)
    other = (B, zh * 2 + 1 - e)

    def mate(i):
        return (half * 8 + i) * 8 + zl, R

    def worked_on(b, j):
        later = jnp.where((b % 4 == 3) & (j >= 1), 1, 0)
        q = 4 * (b % 4) + j
        return task_place((b // 4 + later) % 32, q % 8, q // 8)

    lead = 2 * e + k8 // 4
    gap = k8 % 4
    panel = jnp.where((lead == 3) & (gap >= 1), (4 * t + 127) % 128, 4 * t + lead)
    facing = (panel + gap) % 128

    def o_from(m):
        j = jnp.where(m < 3, 3 - m, m - 3)
        return worked_on(jnp.where(m < 3, (B - j + 128) % 128, B), j)

    barrier = pltpu.get_barrier_semaphore()

    def greet(place):
        unless(
            is_me(place),
            lambda: pl.semaphore_signal(barrier, inc=1, device_id=place, device_id_type=MESH),
        )

    greet(up)
    greet(down)
    greet(other)
    pl.loop(0, 16)(lambda s: greet(a_to(s)))
    pl.loop(0, 8)(lambda s: greet(b_from(s)))
    pl.loop(0, 8)(lambda s: greet(mate(s)))
    pl.loop(0, 7)(lambda s: greet(o_from(s)))
    own_b = jnp.where((z + zl // 4) % 2 == 0, 1, 0)
    own_o = jnp.where((panel == B) | (facing == B), 1, 0)
    out_count = jnp.where(gap == 0, 4, 8)
    pl.semaphore_wait(barrier, 3 + 15 + 8 + 7 + out_count - own_b - own_o)

    @pl.loop(0, 16)
    def _(n):
        k = 2 * ((k8 + n // 2 + z + 4 * (n % 2)) % 8) + n % 2
        send(y_ref.at[k], ra.at[2 * k8 + e], sa_s.at[k], sa_r.at[2 * k8 + e], a_to(k))

    @pl.loop(0, 16)
    def _(n):
        i = (k8 + 32 - z - 4 * e - n // 2) % 8
        s = 2 * i + n % 2
        landed(ra.at[s], sa_r.at[s])
        slot = (zl % 4) * 4 + zh * 2 + n % 2
        send(ra.at[s], rb.at[slot], sb_s.at[s], sb_r.at[slot], b_to(i))

    def fwd_slot(n):
        return jnp.where(n < 4, n, jnp.where(n < 8, n + 8, n - 4))

    @pl.loop(0, 12)
    def _(n):
        s = fwd_slot(n)
        landed(rb.at[s], sb_r.at[s])

        @pl.when(s < 8)
        def _():
            send(rb.at[s], rb.at[16 + s], sf_s.at[s], sf_r.at[s], down)

        @pl.when(s >= 12)
        def _():
            send(rb.at[s], rb.at[12 + s], sf_s.at[s - 4], sf_r.at[s - 4], up)

    pl.loop(8, 12)(lambda s: landed(rb.at[s], sb_r.at[s]))

    def fetch(p):
        x = rb[pl.ds(p * 4, 4)].reshape(256, 256)
        top = x.astype(BF16)
        return x, top, (x - top.astype(F32)).astype(BF16)

    def keep(p, top, rest):
        rows = pl.ds(pl.multiple_of(p * 256, 256), 256)
        xhi[rows, :] = top
        xlo[rows, :] = rest

    def smoothed(p, x, top, rest):
        rows = pl.ds(pl.multiple_of(p * 256, 256), 256)
        beside = jnp.dot(top, adj_ref[...], preferred_element_type=F32)
        beside = beside + jnp.dot(rest, adj_ref[...], preferred_element_type=F32)
        smooth = x * lam_ref[pl.ds(2 * k8 + e, 1), :] + 0.15 * beside
        stop = smooth.astype(BF16)
        shi[rows, :] = stop
        slo[rows, :] = (smooth - stop.astype(F32)).astype(BF16)

    @pl.loop(0, 4)
    def _(p):
        x, top, rest = fetch(p)
        keep(p, top, rest)
        smoothed(p, x, top, rest)

    @pl.loop(0, 2)
    def _(p):
        pl.loop(0, 4)(lambda s: landed(rb.at[16 + p * 4 + s], sf_r.at[p * 4 + s]))
        x, top, rest = fetch(4 + p)
        keep(4 + p, top, rest)

    pl.loop(0, 4)(lambda s: landed(rb.at[24 + s], sf_r.at[8 + s]))
    smoothed(4, *fetch(6))

    def tile(q):
        p, j = q // 4, q % 4
        before = (p == 3) & (j >= 1)
        p, o = jnp.where(before, 4, p), jnp.where(before, j - 1, p + j)
        p = pl.ds(pl.multiple_of(p * 256, 256), 256)
        o = pl.ds(pl.multiple_of(o * 256, 256), 256)
        total = lax.dot_general(shi[p, :], xlo[o, :], NT, preferred_element_type=F32)
        total = total + lax.dot_general(slo[p, :], xhi[o, :], NT, preferred_element_type=F32)
        return total + lax.dot_general(shi[p, :], xhi[o, :], NT, preferred_element_type=F32)

    def turn(n, core):
        return jnp.where(n < 7, (k8 + 1 + (n + 3 * core + 2 * k8) % 7) % 8, k8)

    @pl.loop(0, 8)
    def _(n):
        i = turn(n, 1 - e)
        q = 8 * (1 - e) + i
        part[q] = tile(q)
        send(part.at[q], r1.at[i], s1_s.at[i], s1_r.at[i], other)

    upper, lower = pl.ds(0, 128), pl.ds(128, 128)

    @pl.loop(0, 8)
    def _(n):
        i = turn(n, e)
        q = 8 * e + i
        total = tile(q)
        landed(r1.at[i], s1_r.at[i])
        part[q] = total + r1[i]

        @pl.when(n < 7)
        def _():
            send(part.at[q, upper], r2.at[k8, upper], s2_s.at[i, 0], s2_r.at[k8, 0], mate(i))

    @pl.loop(0, 7)
    def _(n):
        i = turn(n, e)
        send(part.at[8 * e + i, lower], r2.at[k8, lower], s2_s.at[i, 1], s2_r.at[k8, 1], mate(i))

    r2[k8] = part[8 * e + k8]

    for h, rows in enumerate((upper, lower)):

        @pl.loop(0, 7)
        def _(n):
            i = (k8 + 1 + n) % 8
            landed(r2.at[i, rows], s2_r.at[i, h])

        total = r2[0, rows]
        for i in range(1, 8):
            total = total + r2[i, rows]
        across[h] = total.T.reshape(4, 64, 128)
        along[h] = total.reshape(2, 64, 256)

        @pl.loop(0, 4)
        def _(i):
            r = (i + pln) % 4
            send(across.at[h, r], o_ref.at[3 + gap, :, rows], sx_s.at[h, r], so_r.at[3 + gap, h], (panel, r))

        @pl.when(gap >= 1)
        def _():
            @pl.loop(0, 2)
            def _(i):
                send(along.at[h, i], o_ref.at[3 - gap], sy_s.at[h, i], so_r.at[3 - gap, 0], (facing, 2 * h + i))

    pl.loop(0, 3)(lambda m: landed(o_ref.at[m], so_r.at[m, 0]))

    @pl.loop(3, 7)
    def _(m):
        landed(o_ref.at[m, :, upper], so_r.at[m, 0])
        landed(o_ref.at[m, :, lower], so_r.at[m, 1])

    pl.loop(0, 16)(lambda k: sent(y_ref.at[k], sa_s.at[k], a_to(k)))
    pl.loop(0, 16)(lambda s: sent(ra.at[s], sb_s.at[s], b_to(s // 2)))
    pl.loop(0, 8)(lambda s: sent(rb.at[s], sf_s.at[s], down))
    pl.loop(0, 4)(lambda s: sent(rb.at[12 + s], sf_s.at[8 + s], up))
    pl.loop(0, 8)(lambda i: sent(part.at[8 * (1 - e) + i], s1_s.at[i], other))

    for h, rows in enumerate((upper, lower)):
        pl.loop(0, 8)(lambda i: sent(part.at[8 * e + i, rows], s2_s.at[i, h], mate(i)))
        pl.loop(0, 4)(lambda r: sent(across.at[h, r], sx_s.at[h, r], (panel, r)))

        @pl.when(gap >= 1)
        def _():
            pl.loop(0, 2)(lambda i: sent(along.at[h, i], sy_s.at[h, i], (facing, 2 * h + i)))


def band_part(spectral):
    lane = np.arange(128)
    x, layer = lane % 32, lane // 32
    near = np.abs(x[:, None] - x[None, :]) + np.abs(layer[:, None] - layer[None, :]) == 1
    adjacency = jnp.asarray(np.kron(np.eye(2), near), BF16)
    n = np.arange(32)
    lam = 1 + 0.15 * 2 * np.cos(np.pi * (n + 1) / 33)
    lam = jnp.asarray(np.repeat(lam, 128).reshape(16, 256), F32)
    vmem = pl.BlockSpec(memory_space=pltpu.VMEM)
    dma = pltpu.SemaphoreType.DMA
    counts = ((16,),) * 4 + ((12,),) * 2 + ((8,),) * 2 + ((8, 2),) * 2 + ((2, 4), (2, 2), (7, 2))
    return pl.pallas_call(
        band_kernel,
        out_shape=jax.ShapeDtypeStruct((7, 64, 256), F32),
        in_specs=[vmem] * 3,
        out_specs=vmem,
        scratch_shapes=[
            pltpu.VMEM((16, 64, 256), F32),
            pltpu.VMEM((28, 64, 256), F32),
            pltpu.VMEM((1536, 256), BF16),
            pltpu.VMEM((1536, 256), BF16),
            pltpu.VMEM((1280, 256), BF16),
            pltpu.VMEM((1280, 256), BF16),
            pltpu.VMEM((16, 256, 256), F32),
            pltpu.VMEM((8, 256, 256), F32),
            pltpu.VMEM((8, 256, 256), F32),
            pltpu.VMEM((2, 4, 64, 128), F32),
            pltpu.VMEM((2, 2, 64, 256), F32),
        ]
        + [dma(c) for c in counts],
        compiler_params=pltpu.CompilerParams(collective_id=0, has_side_effects=True, vmem_limit_bytes=40 * 2**20),
    )(spectral, lam, adjacency)


def per_device(jacobian, cell_weight, neighbors):
    spectral = local_part(jacobian, cell_weight, neighbors)
    return jnp.swapaxes(band_part(spectral), 1, 2)


def solution(mesh):
    return jax.shard_map(
        per_device,
        mesh=mesh,
        in_specs=(P(("blk", "rep"), None), P(), P()),
        out_specs=P(None, "blk", "rep"),
        check_vma=False,
    )
```

```python
import math

import jax
import jax.numpy as jnp
import numpy as np
from jax import lax
from jax.experimental import pallas as pl
from jax.experimental.pallas import tpu as pltpu
from jax.sharding import PartitionSpec as P

F32, BF16 = jnp.float32, jnp.bfloat16
MESH = pl.DeviceIdType.MESH
SIDE = 32
NT = (((1,), (1,)), ((), ()))


def sine(y, n):
    return math.sqrt(2 / 33) * math.sin(math.pi * (y + 1) * (n + 1) / 33)


def lookup(table_ref, index):
    parts = []
    for g in range(4):
        idx = index[8 * g : 8 * g + 8]
        row, lane = idx >> 7, idx & 127
        out = jnp.zeros((8, 128), jnp.int32)
        for s in range(32):
            line = jnp.broadcast_to(table_ref[s : s + 1, :], (8, 128))
            got = jnp.take_along_axis(line, lane, axis=1, mode="promise_in_bounds")
            out = jnp.where(row == s, got, out)
        parts.append(out)
    return jnp.concatenate(parts, 0)


def steps_to_end(near, rounds, table_ref, own):
    value = jnp.where(near >= 0, near + 4096, own)
    for _ in range(rounds):
        table_ref[...] = value
        index = value & 4095
        value = (value - index) + lookup(table_ref, index)
    return value >> 12


def place_kernel(nb_ref, first, second, table):
    own = lax.broadcasted_iota(jnp.int32, (32, 128), 0) * 128 + lax.broadcasted_iota(jnp.int32, (32, 128), 1)
    missing = [jnp.where(nb_ref[d] < 0, 1.0, 0.0).astype(F32) for d in range(6)]
    count = [jnp.sum(m) for m in missing]

    def pick(flags, arrays):
        total = flags[0] * arrays[0]
        for flag, array in zip(flags[1:], arrays[1:]):
            total = total + flag * array
        return total

    def leading(conds):
        seen, flags = jnp.int32(0), []
        for cond in conds:
            flag = jnp.where(cond, 1, 0) * (1 - seen)
            seen = seen + flag
            flags.append(flag)
        return flags

    nbs = [nb_ref[d] for d in range(6)]
    deep = leading([c > 512.0 for c in count])
    one = leading([c < 512.0 for c in count])
    face = pick([f.astype(F32) for f in one], missing)
    meet = [jnp.sum(face * m) for m in missing]
    two = leading([(c < 512.0) & (m > 0.5) & (f == 0) for c, m, f in zip(count, meet, one)])
    ycoord = steps_to_end(pick(one, nbs), 5, table, own)
    xcoord = steps_to_end(pick(two, nbs), 5, table, own)
    layer = steps_to_end(pick(deep, nbs), 2, table, own)
    first[...] = ycoord >> 2
    second[...] = (ycoord & 3) * 128 + layer * 32 + xcoord


def to_grid_order(j_ref, w_ref, first, second, y_ref, hi, lo, onehot, acc):
    for s in range(32):
        cols = slice(128 * s, 128 * s + 128)
        js = j_ref[:, cols] * w_ref[s : s + 1, :]
        top = js.astype(BF16)
        rest = (js - top.astype(F32)).astype(BF16)
        arow = jnp.broadcast_to(first[s : s + 1, :], (64, 128))
        for a in range(8):
            mask = jnp.where(arow == a, 1.0, 0.0).astype(BF16)
            hi[64 * a : 64 * a + 64, cols] = top * mask
            lo[64 * a : 64 * a + 64, cols] = rest * mask
        brow = jnp.broadcast_to(second[s : s + 1, :], (512, 128))
        onehot[:, cols] = jnp.where(brow == lax.broadcasted_iota(jnp.int32, (512, 128), 0), 1.0, 0.0).astype(BF16)

    for n in range(2):
        part = slice(256 * n, 256 * n + 256)
        acc[:, part] = lax.dot_general(hi[...], onehot[part, :], NT, preferred_element_type=F32) + lax.dot_general(
            lo[...], onehot[part, :], NT, preferred_element_type=F32
        )

    @pl.loop(0, 8)
    def _(g):
        rows = lambda a: pl.ds(pl.multiple_of(a * 64 + g * 8, 8), 8)
        z = lambda y: acc[rows(y // 4), 128 * (y % 4) : 128 * (y % 4) + 128]
        even, odd = [], []
        for y in range(16):
            p, q = z(y), z(31 - y)
            even.append(p + q)
            odd.append(p - q)
        for n in range(32):
            terms = odd if n % 2 else even
            total = terms[0] * sine(0, n)
            for y in range(1, 16):
                total = total + terms[y] * sine(y, n)
            y_ref[n // 2, pl.ds(pl.multiple_of(g * 8, 8), 8), 128 * (n % 2) : 128 * (n % 2) + 128] = total


def places(neighbors):
    vmem = pl.BlockSpec(memory_space=pltpu.VMEM)
    return pl.pallas_call(
        place_kernel,
        out_shape=[jax.ShapeDtypeStruct((32, 128), jnp.int32)] * 2,
        in_specs=[vmem],
        out_specs=[vmem] * 2,
        scratch_shapes=[pltpu.VMEM((32, 128), jnp.int32)],
    )(neighbors.reshape(6, 32, 128))


def task_place(t, k8, e):
    z = t % 16
    return ((t // 16) * 8 + k8) * 8 + z % 8, (z // 8) * 2 + e


def unless(cond, fn):
    pl.when(jnp.logical_not(cond))(fn)


def band_kernel(
    j_ref, w_ref, first, second, lam_ref, adj_ref, o_ref,
    y_ref, hi, lo, onehot, acc,
    ra, rb, xhi, xlo, shi, slo, part, r1, r2, across, along,
    sa_s, sa_r, sb_s, sb_r, sf_s, sf_r, s1_s, s1_r, s2_s, s2_r, sx_s, sy_s, so_r,
):
    B, R = lax.axis_index("blk"), lax.axis_index("rep")
    pln, zl, zh, e = B // 8, B % 8, R // 2, R % 2
    z = zh * 8 + zl
    half, k8 = pln // 8, pln % 8
    t = half * 16 + z

    def is_me(place):
        return (place[0] == B) & (place[1] == R)

    def send(src, dst, s_sem, r_sem, place):
        def there():
            pltpu.make_async_remote_copy(src, dst, s_sem, r_sem, device_id=place, device_id_type=MESH).start()

        def here():
            pltpu.make_async_copy(src, dst, r_sem).start()

        pl.when(is_me(place))(here)
        unless(is_me(place), there)

    def landed(ref, sem):
        pltpu.make_async_copy(ref, ref, sem).wait()

    def sent(ref, sem, place):
        unless(is_me(place), lambda: pltpu.make_async_copy(ref, ref, sem).wait())

    def a_to(k):
        return (half * 8 + k // 2) * 8 + zl, zh * 2 + k % 2

    def b_to(i):
        there = 2 * i + zl // 4
        return pln * 8 + there % 8, (there // 8) * 2 + e

    def b_from(i):
        return pln * 8 + 4 * (z % 2) + i // 2, (i % 2) * 2 + e

    down = task_place((t + 31) % 32, k8, e)
    up = task_place((t + 1) % 32, k8, e)
    other = (B, zh * 2 + 1 - e)

    def mate(i):
        return (half * 8 + i) * 8 + zl, R

    def worked_on(b, j):
        later = jnp.where((b % 4 == 3) & (j >= 1), 1, 0)
        q = 4 * (b % 4) + j
        return task_place((b // 4 + later) % 32, q % 8, q // 8)

    lead = 2 * e + k8 // 4
    gap = k8 % 4
    panel = jnp.where((lead == 3) & (gap >= 1), (4 * t + 127) % 128, 4 * t + lead)
    facing = (panel + gap) % 128

    def o_from(m):
        j = jnp.where(m < 3, 3 - m, m - 3)
        return worked_on(jnp.where(m < 3, (B - j + 128) % 128, B), j)

    barrier = pltpu.get_barrier_semaphore()

    def greet(place):
        unless(
            is_me(place),
            lambda: pl.semaphore_signal(barrier, inc=1, device_id=place, device_id_type=MESH),
        )

    greet(up)
    greet(down)
    greet(other)
    pl.loop(0, 16)(lambda s: greet(a_to(s)))
    pl.loop(0, 8)(lambda s: greet(b_from(s)))
    pl.loop(0, 8)(lambda s: greet(mate(s)))
    pl.loop(0, 7)(lambda s: greet(o_from(s)))
    own_b = jnp.where((z + zl // 4) % 2 == 0, 1, 0)
    own_o = jnp.where((panel == B) | (facing == B), 1, 0)
    out_count = jnp.where(gap == 0, 4, 8)
    to_grid_order(j_ref, w_ref, first, second, y_ref, hi, lo, onehot, acc)
    pl.semaphore_wait(barrier, 3 + 15 + 8 + 7 + out_count - own_b - own_o)

    @pl.loop(0, 16)
    def _(n):
        k = 2 * ((k8 + n // 2 + z + 4 * (n % 2)) % 8) + n % 2
        send(y_ref.at[k], ra.at[2 * k8 + e], sa_s.at[k], sa_r.at[2 * k8 + e], a_to(k))

    @pl.loop(0, 16)
    def _(n):
        i = (k8 + 32 - z - 4 * e - n // 2) % 8
        s = 2 * i + n % 2
        landed(ra.at[s], sa_r.at[s])
        slot = (zl % 4) * 4 + zh * 2 + n % 2
        send(ra.at[s], rb.at[slot], sb_s.at[s], sb_r.at[slot], b_to(i))

    def fwd_slot(n):
        return jnp.where(n < 4, n, jnp.where(n < 8, n + 8, n - 4))

    @pl.loop(0, 12)
    def _(n):
        s = fwd_slot(n)
        landed(rb.at[s], sb_r.at[s])

        @pl.when(s < 8)
        def _():
            send(rb.at[s], rb.at[16 + s], sf_s.at[s], sf_r.at[s], down)

        @pl.when(s >= 12)
        def _():
            send(rb.at[s], rb.at[12 + s], sf_s.at[s - 4], sf_r.at[s - 4], up)

    pl.loop(8, 12)(lambda s: landed(rb.at[s], sb_r.at[s]))

    def fetch(p):
        x = rb[pl.ds(p * 4, 4)].reshape(256, 256)
        top = x.astype(BF16)
        return x, top, (x - top.astype(F32)).astype(BF16)

    def keep(p, top, rest):
        rows = pl.ds(pl.multiple_of(p * 256, 256), 256)
        xhi[rows, :] = top
        xlo[rows, :] = rest

    def smoothed(p, x, top, rest):
        rows = pl.ds(pl.multiple_of(p * 256, 256), 256)
        beside = jnp.dot(top, adj_ref[...], preferred_element_type=F32)
        beside = beside + jnp.dot(rest, adj_ref[...], preferred_element_type=F32)
        smooth = x * lam_ref[pl.ds(2 * k8 + e, 1), :] + 0.15 * beside
        stop = smooth.astype(BF16)
        shi[rows, :] = stop
        slo[rows, :] = (smooth - stop.astype(F32)).astype(BF16)

    @pl.loop(0, 4)
    def _(p):
        x, top, rest = fetch(p)
        keep(p, top, rest)
        smoothed(p, x, top, rest)

    @pl.loop(0, 2)
    def _(p):
        pl.loop(0, 4)(lambda s: landed(rb.at[16 + p * 4 + s], sf_r.at[p * 4 + s]))
        x, top, rest = fetch(4 + p)
        keep(4 + p, top, rest)

    pl.loop(0, 4)(lambda s: landed(rb.at[24 + s], sf_r.at[8 + s]))
    smoothed(4, *fetch(6))

    def tile(q):
        p, j = q // 4, q % 4
        before = (p == 3) & (j >= 1)
        p, o = jnp.where(before, 4, p), jnp.where(before, j - 1, p + j)
        p = pl.ds(pl.multiple_of(p * 256, 256), 256)
        o = pl.ds(pl.multiple_of(o * 256, 256), 256)
        total = lax.dot_general(shi[p, :], xlo[o, :], NT, preferred_element_type=F32)
        total = total + lax.dot_general(slo[p, :], xhi[o, :], NT, preferred_element_type=F32)
        return total + lax.dot_general(shi[p, :], xhi[o, :], NT, preferred_element_type=F32)

    def turn(n, core):
        return jnp.where(n < 7, (k8 + 1 + (n + 3 * core + 2 * k8) % 7) % 8, k8)

    @pl.loop(0, 8)
    def _(n):
        i = turn(n, 1 - e)
        q = 8 * (1 - e) + i
        part[q] = tile(q)
        send(part.at[q], r1.at[i], s1_s.at[i], s1_r.at[i], other)

    upper, lower = pl.ds(0, 128), pl.ds(128, 128)

    @pl.loop(0, 8)
    def _(n):
        i = turn(n, e)
        q = 8 * e + i
        total = tile(q)
        landed(r1.at[i], s1_r.at[i])
        part[q] = total + r1[i]

        @pl.when(n < 7)
        def _():
            send(part.at[q, upper], r2.at[k8, upper], s2_s.at[i, 0], s2_r.at[k8, 0], mate(i))

    r2[k8] = part[8 * e + k8]

    for h, rows in enumerate((upper, lower)):

        @pl.loop(0, 7)
        def _(n):
            i = (k8 + 1 + n) % 8
            landed(r2.at[i, rows], s2_r.at[i, h])

        if h == 0:

            @pl.loop(0, 7)
            def _(n):
                i = turn(n, e)
                send(part.at[8 * e + i, lower], r2.at[k8, lower], s2_s.at[i, 1], s2_r.at[k8, 1], mate(i))

        total = r2[0, rows]
        for i in range(1, 8):
            total = total + r2[i, rows]
        across[h] = total.T.reshape(4, 64, 128)
        along[h] = total.reshape(2, 64, 256)

        @pl.loop(0, 4)
        def _(i):
            r = (i + pln) % 4
            send(across.at[h, r], o_ref.at[3 + gap, :, rows], sx_s.at[h, r], so_r.at[3 + gap, h], (panel, r))

        @pl.when(gap >= 1)
        def _():
            @pl.loop(0, 2)
            def _(i):
                send(along.at[h, i], o_ref.at[3 - gap], sy_s.at[h, i], so_r.at[3 - gap, 0], (facing, 2 * h + i))

    pl.loop(0, 3)(lambda m: landed(o_ref.at[m], so_r.at[m, 0]))

    @pl.loop(3, 7)
    def _(m):
        landed(o_ref.at[m, :, upper], so_r.at[m, 0])
        landed(o_ref.at[m, :, lower], so_r.at[m, 1])

    pl.loop(0, 16)(lambda k: sent(y_ref.at[k], sa_s.at[k], a_to(k)))
    pl.loop(0, 16)(lambda s: sent(ra.at[s], sb_s.at[s], b_to(s // 2)))
    pl.loop(0, 8)(lambda s: sent(rb.at[s], sf_s.at[s], down))
    pl.loop(0, 4)(lambda s: sent(rb.at[12 + s], sf_s.at[8 + s], up))
    pl.loop(0, 8)(lambda i: sent(part.at[8 * (1 - e) + i], s1_s.at[i], other))

    for h, rows in enumerate((upper, lower)):
        pl.loop(0, 8)(lambda i: sent(part.at[8 * e + i, rows], s2_s.at[i, h], mate(i)))
        pl.loop(0, 4)(lambda r: sent(across.at[h, r], sx_s.at[h, r], (panel, r)))

        @pl.when(gap >= 1)
        def _():
            pl.loop(0, 2)(lambda i: sent(along.at[h, i], sy_s.at[h, i], (facing, 2 * h + i)))


def band_part(jacobian, cell_weight, first, second):
    lane = np.arange(128)
    x, layer = lane % 32, lane // 32
    near = np.abs(x[:, None] - x[None, :]) + np.abs(layer[:, None] - layer[None, :]) == 1
    adjacency = jnp.asarray(np.kron(np.eye(2), near), BF16)
    n = np.arange(32)
    lam = 1 + 0.15 * 2 * np.cos(np.pi * (n + 1) / 33)
    lam = jnp.asarray(np.repeat(lam, 128).reshape(16, 256), F32)
    vmem = pl.BlockSpec(memory_space=pltpu.VMEM)
    dma = pltpu.SemaphoreType.DMA
    counts = ((16,),) * 4 + ((12,),) * 2 + ((8,),) * 2 + ((8, 2),) * 2 + ((2, 4), (2, 2), (7, 2))
    return pl.pallas_call(
        band_kernel,
        out_shape=jax.ShapeDtypeStruct((7, 64, 256), F32),
        in_specs=[vmem] * 6,
        out_specs=vmem,
        scratch_shapes=[
            pltpu.VMEM((16, 64, 256), F32),
            pltpu.VMEM((512, 4096), BF16),
            pltpu.VMEM((512, 4096), BF16),
            pltpu.VMEM((512, 4096), BF16),
            pltpu.VMEM((512, 512), F32),
            pltpu.VMEM((16, 64, 256), F32),
            pltpu.VMEM((28, 64, 256), F32),
            pltpu.VMEM((1536, 256), BF16),
            pltpu.VMEM((1536, 256), BF16),
            pltpu.VMEM((1280, 256), BF16),
            pltpu.VMEM((1280, 256), BF16),
            pltpu.VMEM((16, 256, 256), F32),
            pltpu.VMEM((8, 256, 256), F32),
            pltpu.VMEM((8, 256, 256), F32),
            pltpu.VMEM((2, 4, 64, 128), F32),
            pltpu.VMEM((2, 2, 64, 256), F32),
        ]
        + [dma(c) for c in counts],
        compiler_params=pltpu.CompilerParams(collective_id=0, has_side_effects=True, vmem_limit_bytes=48 * 2**20),
    )(jacobian, cell_weight.reshape(32, 128), first, second, lam, adjacency)


def per_device(jacobian, cell_weight, neighbors):
    first, second = places(neighbors)
    return jnp.swapaxes(band_part(jacobian, cell_weight, first, second), 1, 2)


def solution(mesh):
    return jax.shard_map(
        per_device,
        mesh=mesh,
        in_specs=(P(("blk", "rep"), None), P(), P()),
        out_specs=P(None, "blk", "rep"),
        check_vma=False,
    )
```

```python
import math

import jax
import jax.numpy as jnp
import numpy as np
from jax import lax
from jax.experimental import pallas as pl
from jax.experimental.pallas import tpu as pltpu
from jax.sharding import PartitionSpec as P

F32, BF16 = jnp.float32, jnp.bfloat16
MESH = pl.DeviceIdType.MESH
SIDE = 32
NT = (((1,), (1,)), ((), ()))


def sine(y, n):
    return math.sqrt(2 / 33) * math.sin(math.pi * (y + 1) * (n + 1) / 33)


def lookup(table_ref, index):
    parts = []
    for g in range(4):
        idx = index[8 * g : 8 * g + 8]
        row, lane = idx >> 7, idx & 127
        out = jnp.zeros((8, 128), jnp.int32)
        for s in range(32):
            line = jnp.broadcast_to(table_ref[s : s + 1, :], (8, 128))
            got = jnp.take_along_axis(line, lane, axis=1, mode="promise_in_bounds")
            out = jnp.where(row == s, got, out)
        parts.append(out)
    return jnp.concatenate(parts, 0)


def steps_to_end(near, rounds, table_ref, own):
    value = jnp.where(near >= 0, near + 4096, own)
    for _ in range(rounds):
        table_ref[...] = value
        index = value & 4095
        value = (value - index) + lookup(table_ref, index)
    return value >> 12


def place_kernel(rows_ref, first, second, table, nb_ref):
    for s in range(32):
        for d in range(6):
            nb_ref[d, s : s + 1, :] = rows_ref[d : d + 1, 128 * s : 128 * s + 128]
    own = lax.broadcasted_iota(jnp.int32, (32, 128), 0) * 128 + lax.broadcasted_iota(jnp.int32, (32, 128), 1)
    missing = [jnp.where(nb_ref[d] < 0, 1.0, 0.0).astype(F32) for d in range(6)]
    count = [jnp.sum(m) for m in missing]

    def pick(flags, arrays):
        total = flags[0] * arrays[0]
        for flag, array in zip(flags[1:], arrays[1:]):
            total = total + flag * array
        return total

    def leading(conds):
        seen, flags = jnp.int32(0), []
        for cond in conds:
            flag = jnp.where(cond, 1, 0) * (1 - seen)
            seen = seen + flag
            flags.append(flag)
        return flags

    nbs = [nb_ref[d] for d in range(6)]
    deep = leading([c > 512.0 for c in count])
    one = leading([c < 512.0 for c in count])
    face = pick([f.astype(F32) for f in one], missing)
    meet = [jnp.sum(face * m) for m in missing]
    two = leading([(c < 512.0) & (m > 0.5) & (f == 0) for c, m, f in zip(count, meet, one)])
    ycoord = steps_to_end(pick(one, nbs), 5, table, own)
    xcoord = steps_to_end(pick(two, nbs), 5, table, own)
    layer = steps_to_end(pick(deep, nbs), 2, table, own)
    first[...] = ycoord >> 2
    second[...] = (ycoord & 3) * 128 + layer * 32 + xcoord


def to_grid_order(j_ref, w_ref, first, second, y_ref, hi, lo, onehot, acc):
    for s in range(32):
        cols = slice(128 * s, 128 * s + 128)
        js = j_ref[:, cols] * w_ref[s : s + 1, :]
        top = js.astype(BF16)
        rest = (js - top.astype(F32)).astype(BF16)
        arow = jnp.broadcast_to(first[s : s + 1, :], (64, 128))
        for a in range(8):
            mask = jnp.where(arow == a, 1.0, 0.0).astype(BF16)
            hi[64 * a : 64 * a + 64, cols] = top * mask
            lo[64 * a : 64 * a + 64, cols] = rest * mask
        brow = jnp.broadcast_to(second[s : s + 1, :], (512, 128))
        onehot[:, cols] = jnp.where(brow == lax.broadcasted_iota(jnp.int32, (512, 128), 0), 1.0, 0.0).astype(BF16)

    for n in range(2):
        part = slice(256 * n, 256 * n + 256)
        acc[:, part] = lax.dot_general(hi[...], onehot[part, :], NT, preferred_element_type=F32) + lax.dot_general(
            lo[...], onehot[part, :], NT, preferred_element_type=F32
        )

    @pl.loop(0, 8)
    def _(g):
        rows = lambda a: pl.ds(pl.multiple_of(a * 64 + g * 8, 8), 8)
        z = lambda y: acc[rows(y // 4), 128 * (y % 4) : 128 * (y % 4) + 128]
        even, odd = [], []
        for y in range(16):
            p, q = z(y), z(31 - y)
            even.append(p + q)
            odd.append(p - q)
        for n in range(32):
            terms = odd if n % 2 else even
            total = terms[0] * sine(0, n)
            for y in range(1, 16):
                total = total + terms[y] * sine(y, n)
            y_ref[n // 2, pl.ds(pl.multiple_of(g * 8, 8), 8), 128 * (n % 2) : 128 * (n % 2) + 128] = total


def places(neighbors):
    vmem = pl.BlockSpec(memory_space=pltpu.VMEM)
    return pl.pallas_call(
        place_kernel,
        out_shape=[jax.ShapeDtypeStruct((32, 128), jnp.int32)] * 2,
        in_specs=[vmem],
        out_specs=[vmem] * 2,
        scratch_shapes=[pltpu.VMEM((32, 128), jnp.int32), pltpu.VMEM((6, 32, 128), jnp.int32)],
    )(neighbors)


def task_place(t, k8, e):
    z = t % 16
    return ((t // 16) * 8 + k8) * 8 + z % 8, (z // 8) * 2 + e


def unless(cond, fn):
    pl.when(jnp.logical_not(cond))(fn)


def band_kernel(
    far_ref, w_ref, first, second, lam_ref, adj_ref, o_ref,
    j_ref, y_ref, hi, lo, onehot, acc,
    ra, rb, xhi, xlo, shi, slo, part, r1, r2, across, along,
    sa_s, sa_r, sb_s, sb_r, sf_s, sf_r, s1_s, s1_r, s2_s, s2_r, sx_s, sy_s, so_r, j_sem,
):
    B, R = lax.axis_index("blk"), lax.axis_index("rep")
    pln, zl, zh, e = B // 8, B % 8, R // 2, R % 2
    z = zh * 8 + zl
    half, k8 = pln // 8, pln % 8
    t = half * 16 + z

    def is_me(place):
        return (place[0] == B) & (place[1] == R)

    def send(src, dst, s_sem, r_sem, place):
        def there():
            pltpu.make_async_remote_copy(src, dst, s_sem, r_sem, device_id=place, device_id_type=MESH).start()

        def here():
            pltpu.make_async_copy(src, dst, r_sem).start()

        pl.when(is_me(place))(here)
        unless(is_me(place), there)

    def landed(ref, sem):
        pltpu.make_async_copy(ref, ref, sem).wait()

    def sent(ref, sem, place):
        unless(is_me(place), lambda: pltpu.make_async_copy(ref, ref, sem).wait())

    def a_to(k):
        return (half * 8 + k // 2) * 8 + zl, zh * 2 + k % 2

    def b_to(i):
        there = 2 * i + zl // 4
        return pln * 8 + there % 8, (there // 8) * 2 + e

    def b_from(i):
        return pln * 8 + 4 * (z % 2) + i // 2, (i % 2) * 2 + e

    down = task_place((t + 31) % 32, k8, e)
    up = task_place((t + 1) % 32, k8, e)
    other = (B, zh * 2 + 1 - e)

    def mate(i):
        return (half * 8 + i) * 8 + zl, R

    def worked_on(b, j):
        later = jnp.where((b % 4 == 3) & (j >= 1), 1, 0)
        q = 4 * (b % 4) + j
        return task_place((b // 4 + later) % 32, q % 8, q // 8)

    lead = 2 * e + k8 // 4
    gap = k8 % 4
    panel = jnp.where((lead == 3) & (gap >= 1), (4 * t + 127) % 128, 4 * t + lead)
    facing = (panel + gap) % 128

    def o_from(m):
        j = jnp.where(m < 3, 3 - m, m - 3)
        return worked_on(jnp.where(m < 3, (B - j + 128) % 128, B), j)

    fetched = pltpu.make_async_copy(far_ref, j_ref, j_sem.at[0])
    fetched.start()
    barrier = pltpu.get_barrier_semaphore()

    def greet(place):
        unless(
            is_me(place),
            lambda: pl.semaphore_signal(barrier, inc=1, device_id=place, device_id_type=MESH),
        )

    greet(up)
    greet(down)
    greet(other)
    pl.loop(0, 16)(lambda s: greet(a_to(s)))
    pl.loop(0, 8)(lambda s: greet(b_from(s)))
    pl.loop(0, 8)(lambda s: greet(mate(s)))
    pl.loop(0, 7)(lambda s: greet(o_from(s)))
    own_b = jnp.where((z + zl // 4) % 2 == 0, 1, 0)
    own_o = jnp.where((panel == B) | (facing == B), 1, 0)
    out_count = jnp.where(gap == 0, 4, 8)
    fetched.wait()
    to_grid_order(j_ref, w_ref, first, second, y_ref, hi, lo, onehot, acc)
    pl.semaphore_wait(barrier, 3 + 15 + 8 + 7 + out_count - own_b - own_o)

    @pl.loop(0, 16)
    def _(n):
        k = 2 * ((k8 + n // 2 + z + 4 * (n % 2)) % 8) + n % 2
        send(y_ref.at[k], ra.at[2 * k8 + e], sa_s.at[k], sa_r.at[2 * k8 + e], a_to(k))

    @pl.loop(0, 16)
    def _(n):
        i = (k8 + 32 - z - 4 * e - n // 2) % 8
        s = 2 * i + n % 2
        landed(ra.at[s], sa_r.at[s])
        slot = (zl % 4) * 4 + zh * 2 + n % 2
        send(ra.at[s], rb.at[slot], sb_s.at[s], sb_r.at[slot], b_to(i))

    def fwd_slot(n):
        return jnp.where(n < 4, n, jnp.where(n < 8, n + 8, n - 4))

    @pl.loop(0, 12)
    def _(n):
        s = fwd_slot(n)
        landed(rb.at[s], sb_r.at[s])

        @pl.when(s < 8)
        def _():
            send(rb.at[s], rb.at[16 + s], sf_s.at[s], sf_r.at[s], down)

        @pl.when(s >= 12)
        def _():
            send(rb.at[s], rb.at[12 + s], sf_s.at[s - 4], sf_r.at[s - 4], up)

    pl.loop(8, 12)(lambda s: landed(rb.at[s], sb_r.at[s]))

    def fetch(p):
        x = rb[pl.ds(p * 4, 4)].reshape(256, 256)
        top = x.astype(BF16)
        return x, top, (x - top.astype(F32)).astype(BF16)

    def keep(p, top, rest):
        rows = pl.ds(pl.multiple_of(p * 256, 256), 256)
        xhi[rows, :] = top
        xlo[rows, :] = rest

    def smoothed(p, x, top, rest):
        rows = pl.ds(pl.multiple_of(p * 256, 256), 256)
        beside = jnp.dot(top, adj_ref[...], preferred_element_type=F32)
        beside = beside + jnp.dot(rest, adj_ref[...], preferred_element_type=F32)
        smooth = x * lam_ref[pl.ds(2 * k8 + e, 1), :] + 0.15 * beside
        stop = smooth.astype(BF16)
        shi[rows, :] = stop
        slo[rows, :] = (smooth - stop.astype(F32)).astype(BF16)

    @pl.loop(0, 4)
    def _(p):
        x, top, rest = fetch(p)
        keep(p, top, rest)
        smoothed(p, x, top, rest)

    def tile(q):
        p, j = q // 4, q % 4
        before = (p == 3) & (j >= 1)
        p, o = jnp.where(before, 4, p), jnp.where(before, j - 1, p + j)
        p = pl.ds(pl.multiple_of(p * 256, 256), 256)
        o = pl.ds(pl.multiple_of(o * 256, 256), 256)
        total = lax.dot_general(shi[p, :], xlo[o, :], NT, preferred_element_type=F32)
        total = total + lax.dot_general(slo[p, :], xhi[o, :], NT, preferred_element_type=F32)
        return total + lax.dot_general(shi[p, :], xhi[o, :], NT, preferred_element_type=F32)

    def inner(n, core):
        m = (n + k8) % 3
        return jnp.where(core == 0, (n + k8) % 7, m + 2 * (m // 2))

    def outer(n, core):
        m = (n + k8) % 5
        return jnp.where(core == 0, 7, jnp.where(m < 2, m + 2, m + 3))

    def for_other(i):
        q = 8 * (1 - e) + i
        part[q] = tile(q)
        send(part.at[q], r1.at[i], s1_s.at[i], s1_r.at[i], other)

    def for_us(i):
        q = 8 * e + i
        total = tile(q)
        landed(r1.at[i], s1_r.at[i])
        part[q] = total + r1[i]

        @pl.when(i != k8)
        def _():
            send(part.at[q], r2.at[k8], s2_s.at[i], s2_r.at[k8], mate(i))

    pl.loop(0, 3 + 4 * e)(lambda n: for_other(inner(n, 1 - e)))
    pl.loop(0, 7 - 4 * e)(lambda n: for_us(inner(n, e)))

    @pl.loop(0, 2)
    def _(p):
        pl.loop(0, 4)(lambda s: landed(rb.at[16 + p * 4 + s], sf_r.at[p * 4 + s]))
        x, top, rest = fetch(4 + p)
        keep(4 + p, top, rest)

    pl.loop(0, 4)(lambda s: landed(rb.at[24 + s], sf_r.at[8 + s]))
    smoothed(4, *fetch(6))
    pl.loop(0, 5 - 4 * e)(lambda n: for_other(outer(n, 1 - e)))
    pl.loop(0, 1 + 4 * e)(lambda n: for_us(outer(n, e)))
    r2[k8] = part[8 * e + k8]

    @pl.loop(0, 7)
    def _(n):
        i = (k8 + 1 + n) % 8
        landed(r2.at[i], s2_r.at[i])

    total = r2[0]
    for i in range(1, 8):
        total = total + r2[i]
    along[...] = total.reshape(4, 64, 256)
    across[...] = total.T.reshape(4, 64, 256)

    @pl.loop(0, 4)
    def _(i):
        r = (i + pln) % 4
        send(across.at[r], o_ref.at[3 + gap], sx_s.at[r], so_r.at[3 + gap], (panel, r))

        @pl.when(gap >= 1)
        def _():
            send(along.at[r], o_ref.at[3 - gap], sy_s.at[r], so_r.at[3 - gap], (facing, r))

    pl.loop(0, 7)(lambda m: landed(o_ref.at[m], so_r.at[m]))

    pl.loop(0, 16)(lambda k: sent(y_ref.at[k], sa_s.at[k], a_to(k)))
    pl.loop(0, 16)(lambda s: sent(ra.at[s], sb_s.at[s], b_to(s // 2)))
    pl.loop(0, 8)(lambda s: sent(rb.at[s], sf_s.at[s], down))
    pl.loop(0, 4)(lambda s: sent(rb.at[12 + s], sf_s.at[8 + s], up))
    pl.loop(0, 8)(lambda i: sent(part.at[8 * (1 - e) + i], s1_s.at[i], other))
    pl.loop(0, 8)(lambda i: sent(part.at[8 * e + i], s2_s.at[i], mate(i)))
    pl.loop(0, 4)(lambda r: sent(across.at[r], sx_s.at[r], (panel, r)))

    @pl.when(gap >= 1)
    def _():
        pl.loop(0, 4)(lambda r: sent(along.at[r], sy_s.at[r], (facing, r)))


def band_part(jacobian, cell_weight, first, second):
    lane = np.arange(128)
    x, layer = lane % 32, lane // 32
    near = np.abs(x[:, None] - x[None, :]) + np.abs(layer[:, None] - layer[None, :]) == 1
    adjacency = jnp.asarray(np.kron(np.eye(2), near), BF16)
    n = np.arange(32)
    lam = 1 + 0.15 * 2 * np.cos(np.pi * (n + 1) / 33)
    lam = jnp.asarray(np.repeat(lam, 128).reshape(16, 256), F32)
    vmem = pl.BlockSpec(memory_space=pltpu.VMEM)
    dma = pltpu.SemaphoreType.DMA
    counts = ((16,),) * 4 + ((12,),) * 2 + ((8,),) * 4 + ((4,), (4,), (7,), (1,))
    return pl.pallas_call(
        band_kernel,
        out_shape=jax.ShapeDtypeStruct((7, 64, 256), F32),
        in_specs=[pl.BlockSpec(memory_space=pl.ANY)] + [vmem] * 5,
        out_specs=vmem,
        scratch_shapes=[
            pltpu.VMEM((64, 4096), F32),
            pltpu.VMEM((16, 64, 256), F32),
            pltpu.VMEM((512, 4096), BF16),
            pltpu.VMEM((512, 4096), BF16),
            pltpu.VMEM((512, 4096), BF16),
            pltpu.VMEM((512, 512), F32),
            pltpu.VMEM((16, 64, 256), F32),
            pltpu.VMEM((28, 64, 256), F32),
            pltpu.VMEM((1536, 256), BF16),
            pltpu.VMEM((1536, 256), BF16),
            pltpu.VMEM((1280, 256), BF16),
            pltpu.VMEM((1280, 256), BF16),
            pltpu.VMEM((16, 256, 256), F32),
            pltpu.VMEM((8, 256, 256), F32),
            pltpu.VMEM((8, 256, 256), F32),
            pltpu.VMEM((4, 64, 256), F32),
            pltpu.VMEM((4, 64, 256), F32),
        ]
        + [dma(c) for c in counts],
        compiler_params=pltpu.CompilerParams(collective_id=0, has_side_effects=True, vmem_limit_bytes=48 * 2**20),
    )(jacobian, cell_weight.reshape(32, 128), first, second, lam, adjacency)


def per_device(jacobian, cell_weight, neighbors):
    first, second = places(neighbors)
    return jnp.swapaxes(band_part(jacobian, cell_weight, first, second), 1, 2)


def solution(mesh):
    return jax.shard_map(
        per_device,
        mesh=mesh,
        in_specs=(P(("blk", "rep"), None), P(), P()),
        out_specs=P(None, "blk", "rep"),
        check_vma=False,
    )
```

```python
import math

import jax
import jax.numpy as jnp
import numpy as np
from jax import lax
from jax.experimental import pallas as pl
from jax.experimental.pallas import tpu as pltpu
from jax.sharding import PartitionSpec as P

F32, BF16 = jnp.float32, jnp.bfloat16
MESH = pl.DeviceIdType.MESH
SIDE = 32
NT = (((1,), (1,)), ((), ()))


def sine(y, n):
    return math.sqrt(2 / 33) * math.sin(math.pi * (y + 1) * (n + 1) / 33)


def lookup(table_ref, index):
    parts = []
    for g in range(4):
        idx = index[8 * g : 8 * g + 8]
        row, lane = idx >> 7, idx & 127
        out = jnp.zeros((8, 128), jnp.int32)
        for s in range(32):
            line = jnp.broadcast_to(table_ref[s : s + 1, :], (8, 128))
            got = jnp.take_along_axis(line, lane, axis=1, mode="promise_in_bounds")
            out = jnp.where(row == s, got, out)
        parts.append(out)
    return jnp.concatenate(parts, 0)


def steps_to_end(near, rounds, table_ref, own):
    value = jnp.where(near >= 0, near + 4096, own)
    for _ in range(rounds):
        table_ref[...] = value
        index = value & 4095
        value = (value - index) + lookup(table_ref, index)
    return value >> 12


def place_kernel(rows_ref, first, second, table, nb_ref):
    for s in range(32):
        for d in range(6):
            nb_ref[d, s : s + 1, :] = rows_ref[d : d + 1, 128 * s : 128 * s + 128]
    own = lax.broadcasted_iota(jnp.int32, (32, 128), 0) * 128 + lax.broadcasted_iota(jnp.int32, (32, 128), 1)
    missing = [jnp.where(nb_ref[d] < 0, 1.0, 0.0).astype(F32) for d in range(6)]
    count = [jnp.sum(m) for m in missing]

    def pick(flags, arrays):
        total = flags[0] * arrays[0]
        for flag, array in zip(flags[1:], arrays[1:]):
            total = total + flag * array
        return total

    def leading(conds):
        seen, flags = jnp.int32(0), []
        for cond in conds:
            flag = jnp.where(cond, 1, 0) * (1 - seen)
            seen = seen + flag
            flags.append(flag)
        return flags

    nbs = [nb_ref[d] for d in range(6)]
    deep = leading([c > 512.0 for c in count])
    one = leading([c < 512.0 for c in count])
    face = pick([f.astype(F32) for f in one], missing)
    meet = [jnp.sum(face * m) for m in missing]
    two = leading([(c < 512.0) & (m > 0.5) & (f == 0) for c, m, f in zip(count, meet, one)])
    ycoord = steps_to_end(pick(one, nbs), 5, table, own)
    xcoord = steps_to_end(pick(two, nbs), 5, table, own)
    layer = steps_to_end(pick(deep, nbs), 2, table, own)
    first[...] = ycoord >> 2
    second[...] = (ycoord & 3) * 128 + layer * 32 + xcoord


def to_grid_order(j_ref, w_ref, first, second, y_ref, hi, lo, onehot, acc):
    for s in range(32):
        cols = slice(128 * s, 128 * s + 128)
        js = j_ref[:, cols] * w_ref[s : s + 1, :]
        top = js.astype(BF16)
        rest = (js - top.astype(F32)).astype(BF16)
        arow = jnp.broadcast_to(first[s : s + 1, :], (64, 128))
        for a in range(8):
            mask = jnp.where(arow == a, 1.0, 0.0).astype(BF16)
            hi[64 * a : 64 * a + 64, cols] = top * mask
            lo[64 * a : 64 * a + 64, cols] = rest * mask
        brow = jnp.broadcast_to(second[s : s + 1, :], (512, 128))
        onehot[:, cols] = jnp.where(brow == lax.broadcasted_iota(jnp.int32, (512, 128), 0), 1.0, 0.0).astype(BF16)

    for n in range(2):
        part = slice(256 * n, 256 * n + 256)
        acc[:, part] = lax.dot_general(hi[...], onehot[part, :], NT, preferred_element_type=F32) + lax.dot_general(
            lo[...], onehot[part, :], NT, preferred_element_type=F32
        )

    @pl.loop(0, 8)
    def _(g):
        rows = lambda a: pl.ds(pl.multiple_of(a * 64 + g * 8, 8), 8)
        z = lambda y: acc[rows(y // 4), 128 * (y % 4) : 128 * (y % 4) + 128]
        even, odd = [], []
        for y in range(16):
            p, q = z(y), z(31 - y)
            even.append(p + q)
            odd.append(p - q)
        for n in range(32):
            terms = odd if n % 2 else even
            total = terms[0] * sine(0, n)
            for y in range(1, 16):
                total = total + terms[y] * sine(y, n)
            y_ref[n // 2, pl.ds(pl.multiple_of(g * 8, 8), 8), 128 * (n % 2) : 128 * (n % 2) + 128] = total


def places(neighbors):
    vmem = pl.BlockSpec(memory_space=pltpu.VMEM)
    return pl.pallas_call(
        place_kernel,
        out_shape=[jax.ShapeDtypeStruct((32, 128), jnp.int32)] * 2,
        in_specs=[vmem],
        out_specs=[vmem] * 2,
        scratch_shapes=[pltpu.VMEM((32, 128), jnp.int32), pltpu.VMEM((6, 32, 128), jnp.int32)],
    )(neighbors)


def task_place(t, k8, e):
    z = t % 16
    return ((t // 16) * 8 + k8) * 8 + z % 8, (z // 8) * 2 + e


def unless(cond, fn):
    pl.when(jnp.logical_not(cond))(fn)


def band_kernel(
    far_ref, w_ref, first, second, lam_ref, adj_ref, o_ref,
    j_ref, y_ref, hi, lo, onehot, acc,
    ra, rb, xhi, xlo, shi, slo, part, r1, r2, across, along,
    sa_s, sa_r, sb_s, sb_r, sf_s, sf_r, s1_s, s1_r, s2_s, s2_r, sx_s, sy_s, so_r, j_sem,
):
    B, R = lax.axis_index("blk"), lax.axis_index("rep")
    pln, zl, zh, e = B // 8, B % 8, R // 2, R % 2
    z = zh * 8 + zl
    half, k8 = pln // 8, pln % 8
    t = half * 16 + z

    def is_me(place):
        return (place[0] == B) & (place[1] == R)

    def send(src, dst, s_sem, r_sem, place):
        def there():
            pltpu.make_async_remote_copy(src, dst, s_sem, r_sem, device_id=place, device_id_type=MESH).start()

        def here():
            pltpu.make_async_copy(src, dst, r_sem).start()

        pl.when(is_me(place))(here)
        unless(is_me(place), there)

    def landed(ref, sem):
        pltpu.make_async_copy(ref, ref, sem).wait()

    def sent(ref, sem, place):
        unless(is_me(place), lambda: pltpu.make_async_copy(ref, ref, sem).wait())

    def a_to(k):
        return (half * 8 + k // 2) * 8 + zl, zh * 2 + k % 2

    def b_to(i):
        there = 2 * i + zl // 4
        return pln * 8 + there % 8, (there // 8) * 2 + e

    def b_from(i):
        return pln * 8 + 4 * (z % 2) + i // 2, (i % 2) * 2 + e

    down = task_place((t + 31) % 32, k8, e)
    up = task_place((t + 1) % 32, k8, e)
    other = (B, zh * 2 + 1 - e)

    def mate(i):
        return (half * 8 + i) * 8 + zl, R

    def worked_on(b, j):
        later = jnp.where((b % 4 == 3) & (j >= 1), 1, 0)
        q = 4 * (b % 4) + j
        return task_place((b // 4 + later) % 32, q % 8, q // 8)

    lead = 2 * e + k8 // 4
    gap = k8 % 4
    panel = jnp.where((lead == 3) & (gap >= 1), (4 * t + 127) % 128, 4 * t + lead)
    facing = (panel + gap) % 128

    def o_from(m):
        j = jnp.where(m < 3, 3 - m, m - 3)
        return worked_on(jnp.where(m < 3, (B - j + 128) % 128, B), j)

    fetched = pltpu.make_async_copy(far_ref, j_ref, j_sem.at[0])
    fetched.start()
    barrier = pltpu.get_barrier_semaphore()

    def greet(place):
        unless(
            is_me(place),
            lambda: pl.semaphore_signal(barrier, inc=1, device_id=place, device_id_type=MESH),
        )

    greet(up)
    greet(down)
    greet(other)
    pl.loop(0, 16)(lambda s: greet(a_to(s)))
    pl.loop(0, 8)(lambda s: greet(b_from(s)))
    pl.loop(0, 8)(lambda s: greet(mate(s)))
    pl.loop(0, 7)(lambda s: greet(o_from(s)))
    own_b = jnp.where((z + zl // 4) % 2 == 0, 1, 0)
    own_o = jnp.where((panel == B) | (facing == B), 1, 0)
    out_count = jnp.where(gap == 0, 4, 8)
    fetched.wait()
    to_grid_order(j_ref, w_ref, first, second, y_ref, hi, lo, onehot, acc)
    pl.semaphore_wait(barrier, 3 + 15 + 8 + 7 + out_count - own_b - own_o)

    @pl.loop(0, 16)
    def _(n):
        k = 2 * ((k8 + 32 - z // 2 - n // 2 - 4 * (n % 2)) % 8) + n % 2
        send(y_ref.at[k], ra.at[2 * k8 + e], sa_s.at[k], sa_r.at[2 * k8 + e], a_to(k))

    @pl.loop(0, 16)
    def _(n):
        i = (k8 + z // 2 + n // 2 + 4 * e) % 8
        s = 2 * i + n % 2
        landed(ra.at[s], sa_r.at[s])
        slot = (zl % 4) * 4 + zh * 2 + n % 2
        send(ra.at[s], rb.at[slot], sb_s.at[s], sb_r.at[slot], b_to(i))

    def fwd_slot(n):
        return jnp.where(n < 4, n, jnp.where(n < 8, n + 8, n - 4))

    @pl.loop(0, 12)
    def _(n):
        s = fwd_slot(n)
        landed(rb.at[s], sb_r.at[s])

        @pl.when(s < 8)
        def _():
            send(rb.at[s], rb.at[16 + s], sf_s.at[s], sf_r.at[s], down)

        @pl.when(s >= 12)
        def _():
            send(rb.at[s], rb.at[12 + s], sf_s.at[s - 4], sf_r.at[s - 4], up)

    pl.loop(8, 12)(lambda s: landed(rb.at[s], sb_r.at[s]))

    def fetch(p):
        x = rb[pl.ds(p * 4, 4)].reshape(256, 256)
        top = x.astype(BF16)
        return x, top, (x - top.astype(F32)).astype(BF16)

    def keep(p, top, rest):
        rows = pl.ds(pl.multiple_of(p * 256, 256), 256)
        xhi[rows, :] = top
        xlo[rows, :] = rest

    def smoothed(p, x, top, rest):
        rows = pl.ds(pl.multiple_of(p * 256, 256), 256)
        beside = jnp.dot(top, adj_ref[...], preferred_element_type=F32)
        beside = beside + jnp.dot(rest, adj_ref[...], preferred_element_type=F32)
        smooth = x * lam_ref[pl.ds(2 * k8 + e, 1), :] + 0.15 * beside
        stop = smooth.astype(BF16)
        shi[rows, :] = stop
        slo[rows, :] = (smooth - stop.astype(F32)).astype(BF16)

    @pl.loop(0, 4)
    def _(p):
        x, top, rest = fetch(p)
        keep(p, top, rest)
        smoothed(p, x, top, rest)

    def tile(q):
        p, j = q // 4, q % 4
        before = (p == 3) & (j >= 1)
        p, o = jnp.where(before, 4, p), jnp.where(before, j - 1, p + j)
        p = pl.ds(pl.multiple_of(p * 256, 256), 256)
        o = pl.ds(pl.multiple_of(o * 256, 256), 256)
        total = lax.dot_general(shi[p, :], xlo[o, :], NT, preferred_element_type=F32)
        total = total + lax.dot_general(slo[p, :], xhi[o, :], NT, preferred_element_type=F32)
        return total + lax.dot_general(shi[p, :], xhi[o, :], NT, preferred_element_type=F32)

    def inner(n, core):
        m = (n + k8) % 3
        return jnp.where(core == 0, (n + k8) % 7, m + 2 * (m // 2))

    def outer(n, core):
        m = (n + k8) % 5
        return jnp.where(core == 0, 7, jnp.where(m < 2, m + 2, m + 3))

    def for_other(i):
        q = 8 * (1 - e) + i
        part[q] = tile(q)
        send(part.at[q], r1.at[i], s1_s.at[i], s1_r.at[i], other)

    def for_us(i):
        q = 8 * e + i
        total = tile(q)
        landed(r1.at[i], s1_r.at[i])
        part[q] = total + r1[i]

        @pl.when(i != k8)
        def _():
            send(part.at[q], r2.at[k8], s2_s.at[i], s2_r.at[k8], mate(i))

    pl.loop(0, 3 + 4 * e)(lambda n: for_other(inner(n, 1 - e)))
    pl.loop(0, 7 - 4 * e)(lambda n: for_us(inner(n, e)))

    @pl.loop(0, 2)
    def _(p):
        pl.loop(0, 4)(lambda s: landed(rb.at[16 + p * 4 + s], sf_r.at[p * 4 + s]))
        x, top, rest = fetch(4 + p)
        keep(4 + p, top, rest)

    pl.loop(0, 4)(lambda s: landed(rb.at[24 + s], sf_r.at[8 + s]))
    smoothed(4, *fetch(6))
    pl.loop(0, 5 - 4 * e)(lambda n: for_other(outer(n, 1 - e)))
    pl.loop(0, 1 + 4 * e)(lambda n: for_us(outer(n, e)))
    r2[k8] = part[8 * e + k8]

    @pl.loop(0, 7)
    def _(n):
        i = (k8 + 1 + n) % 8
        landed(r2.at[i], s2_r.at[i])

    total = r2[0]
    for i in range(1, 8):
        total = total + r2[i]
    along[...] = total.reshape(4, 64, 256)
    across[...] = total.T.reshape(4, 64, 256)

    @pl.loop(0, 4)
    def _(i):
        r = 2 * ((i + e + z) % 2) + (i // 2 + pln) % 2
        send(across.at[r], o_ref.at[3 + gap], sx_s.at[r], so_r.at[3 + gap], (panel, r))

        @pl.when(gap >= 1)
        def _():
            send(along.at[r], o_ref.at[3 - gap], sy_s.at[r], so_r.at[3 - gap], (facing, r))

    pl.loop(0, 7)(lambda m: landed(o_ref.at[m], so_r.at[m]))

    pl.loop(0, 16)(lambda k: sent(y_ref.at[k], sa_s.at[k], a_to(k)))
    pl.loop(0, 16)(lambda s: sent(ra.at[s], sb_s.at[s], b_to(s // 2)))
    pl.loop(0, 8)(lambda s: sent(rb.at[s], sf_s.at[s], down))
    pl.loop(0, 4)(lambda s: sent(rb.at[12 + s], sf_s.at[8 + s], up))
    pl.loop(0, 8)(lambda i: sent(part.at[8 * (1 - e) + i], s1_s.at[i], other))
    pl.loop(0, 8)(lambda i: sent(part.at[8 * e + i], s2_s.at[i], mate(i)))
    pl.loop(0, 4)(lambda r: sent(across.at[r], sx_s.at[r], (panel, r)))

    @pl.when(gap >= 1)
    def _():
        pl.loop(0, 4)(lambda r: sent(along.at[r], sy_s.at[r], (facing, r)))


def band_part(jacobian, cell_weight, first, second):
    lane = np.arange(128)
    x, layer = lane % 32, lane // 32
    near = np.abs(x[:, None] - x[None, :]) + np.abs(layer[:, None] - layer[None, :]) == 1
    adjacency = jnp.asarray(np.kron(np.eye(2), near), BF16)
    n = np.arange(32)
    lam = 1 + 0.15 * 2 * np.cos(np.pi * (n + 1) / 33)
    lam = jnp.asarray(np.repeat(lam, 128).reshape(16, 256), F32)
    vmem = pl.BlockSpec(memory_space=pltpu.VMEM)
    dma = pltpu.SemaphoreType.DMA
    counts = ((16,),) * 4 + ((12,),) * 2 + ((8,),) * 4 + ((4,), (4,), (7,), (1,))
    return pl.pallas_call(
        band_kernel,
        out_shape=jax.ShapeDtypeStruct((7, 64, 256), F32),
        in_specs=[pl.BlockSpec(memory_space=pl.ANY)] + [vmem] * 5,
        out_specs=vmem,
        scratch_shapes=[
            pltpu.VMEM((64, 4096), F32),
            pltpu.VMEM((16, 64, 256), F32),
            pltpu.VMEM((512, 4096), BF16),
            pltpu.VMEM((512, 4096), BF16),
            pltpu.VMEM((512, 4096), BF16),
            pltpu.VMEM((512, 512), F32),
            pltpu.VMEM((16, 64, 256), F32),
            pltpu.VMEM((28, 64, 256), F32),
            pltpu.VMEM((1536, 256), BF16),
            pltpu.VMEM((1536, 256), BF16),
            pltpu.VMEM((1280, 256), BF16),
            pltpu.VMEM((1280, 256), BF16),
            pltpu.VMEM((16, 256, 256), F32),
            pltpu.VMEM((8, 256, 256), F32),
            pltpu.VMEM((8, 256, 256), F32),
            pltpu.VMEM((4, 64, 256), F32),
            pltpu.VMEM((4, 64, 256), F32),
        ]
        + [dma(c) for c in counts],
        compiler_params=pltpu.CompilerParams(collective_id=0, has_side_effects=True, vmem_limit_bytes=48 * 2**20),
    )(jacobian, cell_weight.reshape(32, 128), first, second, lam, adjacency)


def per_device(jacobian, cell_weight, neighbors):
    first, second = places(neighbors)
    return jnp.swapaxes(band_part(jacobian, cell_weight, first, second), 1, 2)


def solution(mesh):
    return jax.shard_map(
        per_device,
        mesh=mesh,
        in_specs=(P(("blk", "rep"), None), P(), P()),
        out_specs=P(None, "blk", "rep"),
        check_vma=False,
    )
```

```python
import math

import jax
import jax.numpy as jnp
import numpy as np
from jax import lax
from jax.experimental import pallas as pl
from jax.experimental.pallas import tpu as pltpu
from jax.sharding import PartitionSpec as P

F32, BF16 = jnp.float32, jnp.bfloat16
MESH = pl.DeviceIdType.MESH
SIDE = 32
NT = (((1,), (1,)), ((), ()))


def sine(y, n):
    return math.sqrt(2 / 33) * math.sin(math.pi * (y + 1) * (n + 1) / 33)


def lookup(table_ref, index):
    parts = []
    for g in range(4):
        idx = index[8 * g : 8 * g + 8]
        row, lane = idx >> 7, idx & 127
        out = jnp.zeros((8, 128), jnp.int32)
        for s in range(32):
            line = jnp.broadcast_to(table_ref[s : s + 1, :], (8, 128))
            got = jnp.take_along_axis(line, lane, axis=1, mode="promise_in_bounds")
            out = jnp.where(row == s, got, out)
        parts.append(out)
    return jnp.concatenate(parts, 0)


def steps_to_end(near, rounds, table_ref, own):
    value = jnp.where(near >= 0, near + 4096, own)
    for _ in range(rounds):
        table_ref[...] = value
        index = value & 4095
        value = (value - index) + lookup(table_ref, index)
    return value >> 12


def place_kernel(rows_ref, first, second, table, nb_ref):
    for s in range(32):
        for d in range(6):
            nb_ref[d, s : s + 1, :] = rows_ref[d : d + 1, 128 * s : 128 * s + 128]
    own = lax.broadcasted_iota(jnp.int32, (32, 128), 0) * 128 + lax.broadcasted_iota(jnp.int32, (32, 128), 1)
    missing = [jnp.where(nb_ref[d] < 0, 1.0, 0.0).astype(F32) for d in range(6)]
    count = [jnp.sum(m) for m in missing]

    def pick(flags, arrays):
        total = flags[0] * arrays[0]
        for flag, array in zip(flags[1:], arrays[1:]):
            total = total + flag * array
        return total

    def leading(conds):
        seen, flags = jnp.int32(0), []
        for cond in conds:
            flag = jnp.where(cond, 1, 0) * (1 - seen)
            seen = seen + flag
            flags.append(flag)
        return flags

    nbs = [nb_ref[d] for d in range(6)]
    deep = leading([c > 512.0 for c in count])
    one = leading([c < 512.0 for c in count])
    face = pick([f.astype(F32) for f in one], missing)
    meet = [jnp.sum(face * m) for m in missing]
    two = leading([(c < 512.0) & (m > 0.5) & (f == 0) for c, m, f in zip(count, meet, one)])
    ycoord = steps_to_end(pick(one, nbs), 5, table, own)
    xcoord = steps_to_end(pick(two, nbs), 5, table, own)
    layer = steps_to_end(pick(deep, nbs), 2, table, own)
    first[...] = ycoord >> 2
    second[...] = (ycoord & 3) * 128 + layer * 32 + xcoord


def to_grid_order(j_ref, w_ref, first, second, y_ref, hi, lo, onehot, acc):
    for s in range(32):
        cols = slice(128 * s, 128 * s + 128)
        js = j_ref[:, cols] * w_ref[s : s + 1, :]
        top = js.astype(BF16)
        rest = (js - top.astype(F32)).astype(BF16)
        arow = jnp.broadcast_to(first[s : s + 1, :], (64, 128))
        for a in range(8):
            mask = jnp.where(arow == a, 1.0, 0.0).astype(BF16)
            hi[64 * a : 64 * a + 64, cols] = top * mask
            lo[64 * a : 64 * a + 64, cols] = rest * mask
        brow = jnp.broadcast_to(second[s : s + 1, :], (512, 128))
        onehot[:, cols] = jnp.where(brow == lax.broadcasted_iota(jnp.int32, (512, 128), 0), 1.0, 0.0).astype(BF16)

    for n in range(2):
        part = slice(256 * n, 256 * n + 256)
        acc[:, part] = lax.dot_general(hi[...], onehot[part, :], NT, preferred_element_type=F32) + lax.dot_general(
            lo[...], onehot[part, :], NT, preferred_element_type=F32
        )

    @pl.loop(0, 8)
    def _(g):
        rows = lambda a: pl.ds(pl.multiple_of(a * 64 + g * 8, 8), 8)
        z = lambda y: acc[rows(y // 4), 128 * (y % 4) : 128 * (y % 4) + 128]
        even, odd = [], []
        for y in range(16):
            p, q = z(y), z(31 - y)
            even.append(p + q)
            odd.append(p - q)
        for n in range(32):
            terms = odd if n % 2 else even
            total = terms[0] * sine(0, n)
            for y in range(1, 16):
                total = total + terms[y] * sine(y, n)
            y_ref[n // 2, pl.ds(pl.multiple_of(g * 8, 8), 8), 128 * (n % 2) : 128 * (n % 2) + 128] = total


def places(neighbors):
    vmem = pl.BlockSpec(memory_space=pltpu.VMEM)
    return pl.pallas_call(
        place_kernel,
        out_shape=[jax.ShapeDtypeStruct((32, 128), jnp.int32)] * 2,
        in_specs=[vmem],
        out_specs=[vmem] * 2,
        scratch_shapes=[pltpu.VMEM((32, 128), jnp.int32), pltpu.VMEM((6, 32, 128), jnp.int32)],
    )(neighbors)


def task_place(t, k8, e):
    z = t % 16
    return ((t // 16) * 8 + k8) * 8 + z % 8, (z // 8) * 2 + e


def unless(cond, fn):
    pl.when(jnp.logical_not(cond))(fn)


def band_kernel(
    far_ref, w_ref, first, second, lam_ref, adj_ref, o_ref,
    j_ref, y_ref, hi, lo, onehot, acc,
    ra, rb, xhi, xlo, shi, slo, part, r1, r2, across, along,
    sa_s, sa_r, sb_s, sb_r, sf_s, sf_r, s1_s, s1_r, s2_s, s2_r, sx_s, sy_s, so_r, j_sem,
):
    B, R = lax.axis_index("blk"), lax.axis_index("rep")
    pln, zl, zh, e = B // 8, B % 8, R // 2, R % 2
    z = zh * 8 + zl
    half, k8 = pln // 8, pln % 8
    t = half * 16 + z

    def is_me(place):
        return (place[0] == B) & (place[1] == R)

    def send(src, dst, s_sem, r_sem, place):
        def there():
            pltpu.make_async_remote_copy(src, dst, s_sem, r_sem, device_id=place, device_id_type=MESH).start()

        def here():
            pltpu.make_async_copy(src, dst, r_sem).start()

        pl.when(is_me(place))(here)
        unless(is_me(place), there)

    def landed(ref, sem):
        pltpu.make_async_copy(ref, ref, sem).wait()

    def sent(ref, sem, place):
        unless(is_me(place), lambda: pltpu.make_async_copy(ref, ref, sem).wait())

    def a_to(k):
        return (half * 8 + k // 2) * 8 + zl, zh * 2 + k % 2

    def b_to(i):
        there = 2 * i + zl // 4
        return pln * 8 + there % 8, (there // 8) * 2 + e

    def b_from(i):
        return pln * 8 + 4 * (z % 2) + i // 2, (i % 2) * 2 + e

    down = task_place((t + 31) % 32, k8, e)
    up = task_place((t + 1) % 32, k8, e)
    other = (B, zh * 2 + 1 - e)

    def mate(i):
        return (half * 8 + i) * 8 + zl, R

    def worked_on(b, j):
        later = jnp.where((b % 4 == 3) & (j >= 1), 1, 0)
        q = 4 * (b % 4) + j
        return task_place((b // 4 + later) % 32, q % 8, q // 8)

    lead = 2 * e + k8 // 4
    gap = k8 % 4
    panel = jnp.where((lead == 3) & (gap >= 1), (4 * t + 127) % 128, 4 * t + lead)
    facing = (panel + gap) % 128

    def o_from(m):
        j = jnp.where(m < 3, 3 - m, m - 3)
        return worked_on(jnp.where(m < 3, (B - j + 128) % 128, B), j)

    fetched = pltpu.make_async_copy(far_ref, j_ref, j_sem.at[0])
    fetched.start()
    barrier = pltpu.get_barrier_semaphore()

    def greet(place):
        unless(
            is_me(place),
            lambda: pl.semaphore_signal(barrier, inc=1, device_id=place, device_id_type=MESH),
        )

    greet(up)
    greet(down)
    greet(other)
    pl.loop(0, 16)(lambda s: greet(a_to(s)))
    pl.loop(0, 8)(lambda s: greet(b_from(s)))
    pl.loop(0, 8)(lambda s: greet(mate(s)))
    pl.loop(0, 7)(lambda s: greet(o_from(s)))
    own_b = jnp.where((z + zl // 4) % 2 == 0, 1, 0)
    own_o = jnp.where((panel == B) | (facing == B), 1, 0)
    out_count = jnp.where(gap == 0, 4, 8)
    fetched.wait()
    to_grid_order(j_ref, w_ref, first, second, y_ref, hi, lo, onehot, acc)
    pl.semaphore_wait(barrier, 3 + 15 + 8 + 7 + out_count - own_b - own_o)

    @pl.loop(0, 16)
    def _(n):
        k = 2 * ((k8 + n // 2 + z + 4 * (n % 2)) % 8) + n % 2
        send(y_ref.at[k], ra.at[2 * k8 + e], sa_s.at[k], sa_r.at[2 * k8 + e], a_to(k))

    @pl.loop(0, 16)
    def _(n):
        i = (k8 + 32 - z - 4 * e - n // 2) % 8
        s = 2 * i + n % 2
        landed(ra.at[s], sa_r.at[s])
        slot = (zl % 4) * 4 + zh * 2 + n % 2
        send(ra.at[s], rb.at[slot], sb_s.at[s], sb_r.at[slot], b_to(i))

    def fwd_slot(n):
        return jnp.where(n < 4, n, jnp.where(n < 8, n + 8, n - 4))

    @pl.loop(0, 12)
    def _(n):
        s = fwd_slot(n)
        landed(rb.at[s], sb_r.at[s])

        @pl.when(s < 8)
        def _():
            send(rb.at[s], rb.at[16 + s], sf_s.at[s], sf_r.at[s], down)

        @pl.when(s >= 12)
        def _():
            send(rb.at[s], rb.at[12 + s], sf_s.at[s - 4], sf_r.at[s - 4], up)

    pl.loop(8, 12)(lambda s: landed(rb.at[s], sb_r.at[s]))

    def fetch(p):
        x = rb[pl.ds(p * 4, 4)].reshape(256, 256)
        top = x.astype(BF16)
        return x, top, (x - top.astype(F32)).astype(BF16)

    def keep(p, top, rest):
        rows = pl.ds(pl.multiple_of(p * 256, 256), 256)
        xhi[rows, :] = top
        xlo[rows, :] = rest

    def smoothed(p, x, top, rest):
        rows = pl.ds(pl.multiple_of(p * 256, 256), 256)
        beside = jnp.dot(top, adj_ref[...], preferred_element_type=F32)
        beside = beside + jnp.dot(rest, adj_ref[...], preferred_element_type=F32)
        smooth = x * lam_ref[pl.ds(2 * k8 + e, 1), :] + 0.15 * beside
        stop = smooth.astype(BF16)
        shi[rows, :] = stop
        slo[rows, :] = (smooth - stop.astype(F32)).astype(BF16)

    @pl.loop(0, 4)
    def _(p):
        x, top, rest = fetch(p)
        keep(p, top, rest)
        smoothed(p, x, top, rest)

    def tile(q):
        p, j = q // 4, q % 4
        before = (p == 3) & (j >= 1)
        p, o = jnp.where(before, 4, p), jnp.where(before, j - 1, p + j)
        p = pl.ds(pl.multiple_of(p * 256, 256), 256)
        o = pl.ds(pl.multiple_of(o * 256, 256), 256)
        total = lax.dot_general(shi[p, :], xlo[o, :], NT, preferred_element_type=F32)
        total = total + lax.dot_general(slo[p, :], xhi[o, :], NT, preferred_element_type=F32)
        return total + lax.dot_general(shi[p, :], xhi[o, :], NT, preferred_element_type=F32)

    def inner(n, core):
        m = (n + 2 * k8) % 3
        return jnp.where(core == 0, (n + 3 * k8) % 7, m + 2 * (m // 2))

    def outer(n, core):
        m = (n + 3 * k8) % 5
        return jnp.where(core == 0, 7, jnp.where(m < 2, m + 2, m + 3))

    def for_other(i):
        q = 8 * (1 - e) + i
        part[q] = tile(q)
        send(part.at[q], r1.at[i], s1_s.at[i], s1_r.at[i], other)

    def for_us(i):
        q = 8 * e + i
        total = tile(q)
        landed(r1.at[i], s1_r.at[i])
        part[q] = total + r1[i]

        @pl.when(i != k8)
        def _():
            send(part.at[q], r2.at[k8], s2_s.at[i], s2_r.at[k8], mate(i))

    pl.loop(0, 3 + 4 * e)(lambda n: for_other(inner(n, 1 - e)))
    pl.loop(0, 7 - 4 * e)(lambda n: for_us(inner(n, e)))

    @pl.loop(0, 2)
    def _(p):
        pl.loop(0, 4)(lambda s: landed(rb.at[16 + p * 4 + s], sf_r.at[p * 4 + s]))
        x, top, rest = fetch(4 + p)
        keep(4 + p, top, rest)

    pl.loop(0, 4)(lambda s: landed(rb.at[24 + s], sf_r.at[8 + s]))
    smoothed(4, *fetch(6))
    pl.loop(0, 5 - 4 * e)(lambda n: for_other(outer(n, 1 - e)))
    pl.loop(0, 1 + 4 * e)(lambda n: for_us(outer(n, e)))
    r2[k8] = part[8 * e + k8]

    @pl.loop(0, 7)
    def _(n):
        i = (k8 + 1 + n) % 8
        landed(r2.at[i], s2_r.at[i])

    total = r2[0]
    for i in range(1, 8):
        total = total + r2[i]
    along[...] = total.reshape(4, 64, 256)
    across[...] = total.T.reshape(4, 64, 256)

    @pl.loop(0, 4)
    def _(i):
        r = 2 * ((i + e + z) % 2) + (i // 2 + pln) % 2
        send(across.at[r], o_ref.at[3 + gap], sx_s.at[r], so_r.at[3 + gap], (panel, r))

        @pl.when(gap >= 1)
        def _():
            send(along.at[r], o_ref.at[3 - gap], sy_s.at[r], so_r.at[3 - gap], (facing, r))

    pl.loop(0, 7)(lambda m: landed(o_ref.at[m], so_r.at[m]))

    pl.loop(0, 16)(lambda k: sent(y_ref.at[k], sa_s.at[k], a_to(k)))
    pl.loop(0, 16)(lambda s: sent(ra.at[s], sb_s.at[s], b_to(s // 2)))
    pl.loop(0, 8)(lambda s: sent(rb.at[s], sf_s.at[s], down))
    pl.loop(0, 4)(lambda s: sent(rb.at[12 + s], sf_s.at[8 + s], up))
    pl.loop(0, 8)(lambda i: sent(part.at[8 * (1 - e) + i], s1_s.at[i], other))
    pl.loop(0, 8)(lambda i: sent(part.at[8 * e + i], s2_s.at[i], mate(i)))
    pl.loop(0, 4)(lambda r: sent(across.at[r], sx_s.at[r], (panel, r)))

    @pl.when(gap >= 1)
    def _():
        pl.loop(0, 4)(lambda r: sent(along.at[r], sy_s.at[r], (facing, r)))


def band_part(jacobian, cell_weight, first, second):
    lane = np.arange(128)
    x, layer = lane % 32, lane // 32
    near = np.abs(x[:, None] - x[None, :]) + np.abs(layer[:, None] - layer[None, :]) == 1
    adjacency = jnp.asarray(np.kron(np.eye(2), near), BF16)
    n = np.arange(32)
    lam = 1 + 0.15 * 2 * np.cos(np.pi * (n + 1) / 33)
    lam = jnp.asarray(np.repeat(lam, 128).reshape(16, 256), F32)
    vmem = pl.BlockSpec(memory_space=pltpu.VMEM)
    dma = pltpu.SemaphoreType.DMA
    counts = ((16,),) * 4 + ((12,),) * 2 + ((8,),) * 4 + ((4,), (4,), (7,), (1,))
    return pl.pallas_call(
        band_kernel,
        out_shape=jax.ShapeDtypeStruct((7, 64, 256), F32),
        in_specs=[pl.BlockSpec(memory_space=pl.ANY)] + [vmem] * 5,
        out_specs=vmem,
        scratch_shapes=[
            pltpu.VMEM((64, 4096), F32),
            pltpu.VMEM((16, 64, 256), F32),
            pltpu.VMEM((512, 4096), BF16),
            pltpu.VMEM((512, 4096), BF16),
            pltpu.VMEM((512, 4096), BF16),
            pltpu.VMEM((512, 512), F32),
            pltpu.VMEM((16, 64, 256), F32),
            pltpu.VMEM((28, 64, 256), F32),
            pltpu.VMEM((1536, 256), BF16),
            pltpu.VMEM((1536, 256), BF16),
            pltpu.VMEM((1280, 256), BF16),
            pltpu.VMEM((1280, 256), BF16),
            pltpu.VMEM((16, 256, 256), F32),
            pltpu.VMEM((8, 256, 256), F32),
            pltpu.VMEM((8, 256, 256), F32),
            pltpu.VMEM((4, 64, 256), F32),
            pltpu.VMEM((4, 64, 256), F32),
        ]
        + [dma(c) for c in counts],
        compiler_params=pltpu.CompilerParams(collective_id=0, has_side_effects=True, vmem_limit_bytes=48 * 2**20),
    )(jacobian, cell_weight.reshape(32, 128), first, second, lam, adjacency)


def per_device(jacobian, cell_weight, neighbors):
    first, second = places(neighbors)
    return jnp.swapaxes(band_part(jacobian, cell_weight, first, second), 1, 2)


def solution(mesh):
    return jax.shard_map(
        per_device,
        mesh=mesh,
        in_specs=(P(("blk", "rep"), None), P(), P()),
        out_specs=P(None, "blk", "rep"),
        check_vma=False,
    )
```

```python
import math

import jax
import jax.numpy as jnp
import numpy as np
from jax import lax
from jax.experimental import pallas as pl
from jax.experimental.pallas import tpu as pltpu
from jax.sharding import PartitionSpec as P

F32, BF16 = jnp.float32, jnp.bfloat16
MESH = pl.DeviceIdType.MESH
SIDE = 32
NT = (((1,), (1,)), ((), ()))


def sine(y, n):
    return math.sqrt(2 / 33) * math.sin(math.pi * (y + 1) * (n + 1) / 33)


def lookup(table_ref, index):
    parts = []
    for g in range(4):
        idx = index[8 * g : 8 * g + 8]
        row, lane = idx >> 7, idx & 127
        out = jnp.zeros((8, 128), jnp.int32)
        for s in range(32):
            line = jnp.broadcast_to(table_ref[s : s + 1, :], (8, 128))
            got = jnp.take_along_axis(line, lane, axis=1, mode="promise_in_bounds")
            out = jnp.where(row == s, got, out)
        parts.append(out)
    return jnp.concatenate(parts, 0)


def steps_to_end(near, rounds, table_ref, own):
    value = jnp.where(near >= 0, near + 4096, own)
    for _ in range(rounds):
        table_ref[...] = value
        index = value & 4095
        value = (value - index) + lookup(table_ref, index)
    return value >> 12


def place_kernel(rows_ref, first, second, table, nb_ref):
    for s in range(32):
        for d in range(6):
            nb_ref[d, s : s + 1, :] = rows_ref[d : d + 1, 128 * s : 128 * s + 128]
    own = lax.broadcasted_iota(jnp.int32, (32, 128), 0) * 128 + lax.broadcasted_iota(jnp.int32, (32, 128), 1)
    missing = [jnp.where(nb_ref[d] < 0, 1.0, 0.0).astype(F32) for d in range(6)]
    count = [jnp.sum(m) for m in missing]

    def pick(flags, arrays):
        total = flags[0] * arrays[0]
        for flag, array in zip(flags[1:], arrays[1:]):
            total = total + flag * array
        return total

    def leading(conds):
        seen, flags = jnp.int32(0), []
        for cond in conds:
            flag = jnp.where(cond, 1, 0) * (1 - seen)
            seen = seen + flag
            flags.append(flag)
        return flags

    nbs = [nb_ref[d] for d in range(6)]
    deep = leading([c > 512.0 for c in count])
    one = leading([c < 512.0 for c in count])
    face = pick([f.astype(F32) for f in one], missing)
    meet = [jnp.sum(face * m) for m in missing]
    two = leading([(c < 512.0) & (m > 0.5) & (f == 0) for c, m, f in zip(count, meet, one)])
    ycoord = steps_to_end(pick(one, nbs), 5, table, own)
    xcoord = steps_to_end(pick(two, nbs), 5, table, own)
    layer = steps_to_end(pick(deep, nbs), 2, table, own)
    first[...] = ycoord >> 2
    second[...] = (ycoord & 3) * 128 + layer * 32 + xcoord


def to_grid_order(j_ref, w_ref, first, second, y_ref, hi, lo, onehot, acc):
    for s in range(32):
        cols = slice(128 * s, 128 * s + 128)
        js = j_ref[:, cols] * w_ref[s : s + 1, :]
        top = js.astype(BF16)
        rest = (js - top.astype(F32)).astype(BF16)
        arow = jnp.broadcast_to(first[s : s + 1, :], (64, 128))
        for a in range(8):
            mask = jnp.where(arow == a, 1.0, 0.0).astype(BF16)
            hi[64 * a : 64 * a + 64, cols] = top * mask
            lo[64 * a : 64 * a + 64, cols] = rest * mask
        brow = jnp.broadcast_to(second[s : s + 1, :], (512, 128))
        onehot[:, cols] = jnp.where(brow == lax.broadcasted_iota(jnp.int32, (512, 128), 0), 1.0, 0.0).astype(BF16)

    for n in range(2):
        part = slice(256 * n, 256 * n + 256)
        acc[:, part] = lax.dot_general(hi[...], onehot[part, :], NT, preferred_element_type=F32) + lax.dot_general(
            lo[...], onehot[part, :], NT, preferred_element_type=F32
        )

    @pl.loop(0, 8)
    def _(g):
        rows = lambda a: pl.ds(pl.multiple_of(a * 64 + g * 8, 8), 8)
        z = lambda y: acc[rows(y // 4), 128 * (y % 4) : 128 * (y % 4) + 128]
        even, odd = [], []
        for y in range(16):
            p, q = z(y), z(31 - y)
            even.append(p + q)
            odd.append(p - q)
        for n in range(32):
            terms = odd if n % 2 else even
            total = terms[0] * sine(0, n)
            for y in range(1, 16):
                total = total + terms[y] * sine(y, n)
            y_ref[n // 2, pl.ds(pl.multiple_of(g * 8, 8), 8), 128 * (n % 2) : 128 * (n % 2) + 128] = total


def places(neighbors):
    vmem = pl.BlockSpec(memory_space=pltpu.VMEM)
    return pl.pallas_call(
        place_kernel,
        out_shape=[jax.ShapeDtypeStruct((32, 128), jnp.int32)] * 2,
        in_specs=[vmem],
        out_specs=[vmem] * 2,
        scratch_shapes=[pltpu.VMEM((32, 128), jnp.int32), pltpu.VMEM((6, 32, 128), jnp.int32)],
    )(neighbors)


def task_place(t, k8, e):
    z = t % 16
    return ((t // 16) * 8 + k8) * 8 + z % 8, (z // 8) * 2 + e


def unless(cond, fn):
    pl.when(jnp.logical_not(cond))(fn)


def band_kernel(
    far_j, far_w, far_first, far_second, far_lam, far_adj, o_ref,
    j_ref, w_ref, first, second, lam_ref, adj_ref, y_ref, hi, lo, onehot, acc,
    ra, rb, xhi, xlo, shi, slo, part, r1, r2, across, along,
    sa_s, sa_r, sb_s, sb_r, sf_s, sf_r, s1_s, s1_r, s2_s, s2_r, sx_s, sy_s, so_r, in_sem,
):
    B, R = lax.axis_index("blk"), lax.axis_index("rep")
    pln, zl, zh, e = B // 8, B % 8, R // 2, R % 2
    z = zh * 8 + zl
    half, k8 = pln // 8, pln % 8
    t = half * 16 + z

    def is_me(place):
        return (place[0] == B) & (place[1] == R)

    def send(src, dst, s_sem, r_sem, place):
        def there():
            pltpu.make_async_remote_copy(src, dst, s_sem, r_sem, device_id=place, device_id_type=MESH).start()

        def here():
            pltpu.make_async_copy(src, dst, r_sem).start()

        pl.when(is_me(place))(here)
        unless(is_me(place), there)

    def landed(ref, sem):
        pltpu.make_async_copy(ref, ref, sem).wait()

    def sent(ref, sem, place):
        unless(is_me(place), lambda: pltpu.make_async_copy(ref, ref, sem).wait())

    def a_to(k):
        return (half * 8 + k // 2) * 8 + zl, zh * 2 + k % 2

    def b_to(i):
        there = 2 * i + zl // 4
        return pln * 8 + there % 8, (there // 8) * 2 + e

    def b_from(i):
        return pln * 8 + 4 * (z % 2) + i // 2, (i % 2) * 2 + e

    down = task_place((t + 31) % 32, k8, e)
    up = task_place((t + 1) % 32, k8, e)
    other = (B, zh * 2 + 1 - e)

    def mate(i):
        return (half * 8 + i) * 8 + zl, R

    def worked_on(b, j):
        later = jnp.where((b % 4 == 3) & (j >= 1), 1, 0)
        q = 4 * (b % 4) + j
        return task_place((b // 4 + later) % 32, q % 8, q // 8)

    lead = 2 * e + k8 // 4
    gap = k8 % 4
    panel = jnp.where((lead == 3) & (gap >= 1), (4 * t + 127) % 128, 4 * t + lead)
    facing = (panel + gap) % 128

    def o_from(m):
        j = jnp.where(m < 3, 3 - m, m - 3)
        return worked_on(jnp.where(m < 3, (B - j + 128) % 128, B), j)

    fetched = [
        pltpu.make_async_copy(far, near, in_sem.at[i])
        for i, (far, near) in enumerate(
            (
                (far_j, j_ref), (far_w, w_ref), (far_first, first),
                (far_second, second), (far_lam, lam_ref), (far_adj, adj_ref),
            )
        )
    ]
    for copy in fetched:
        copy.start()
    barrier = pltpu.get_barrier_semaphore()

    def greet(place):
        unless(
            is_me(place),
            lambda: pl.semaphore_signal(barrier, inc=1, device_id=place, device_id_type=MESH),
        )

    greet(up)
    greet(down)
    greet(other)
    pl.loop(0, 16)(lambda s: greet(a_to(s)))
    pl.loop(0, 8)(lambda s: greet(b_from(s)))
    pl.loop(0, 8)(lambda s: greet(mate(s)))
    pl.loop(0, 7)(lambda s: greet(o_from(s)))
    own_b = jnp.where((z + zl // 4) % 2 == 0, 1, 0)
    own_o = jnp.where((panel == B) | (facing == B), 1, 0)
    out_count = jnp.where(gap == 0, 4, 8)
    for copy in fetched:
        copy.wait()
    to_grid_order(j_ref, w_ref, first, second, y_ref, hi, lo, onehot, acc)
    pl.semaphore_wait(barrier, 3 + 15 + 8 + 7 + out_count - own_b - own_o)

    @pl.loop(0, 16)
    def _(n):
        k = 2 * ((k8 + n // 2 + z + 4 * (n % 2)) % 8) + n % 2
        send(y_ref.at[k], ra.at[2 * k8 + e], sa_s.at[k], sa_r.at[2 * k8 + e], a_to(k))

    @pl.loop(0, 16)
    def _(n):
        i = (k8 + 32 - z - 4 * e - n // 2) % 8
        s = 2 * i + n % 2
        landed(ra.at[s], sa_r.at[s])
        slot = (zl % 4) * 4 + zh * 2 + n % 2
        send(ra.at[s], rb.at[slot], sb_s.at[s], sb_r.at[slot], b_to(i))

    def fwd_slot(n):
        return jnp.where(n < 4, n, jnp.where(n < 8, n + 8, n - 4))

    @pl.loop(0, 12)
    def _(n):
        s = fwd_slot(n)
        landed(rb.at[s], sb_r.at[s])

        @pl.when(s < 8)
        def _():
            send(rb.at[s], rb.at[16 + s], sf_s.at[s], sf_r.at[s], down)

        @pl.when(s >= 12)
        def _():
            send(rb.at[s], rb.at[12 + s], sf_s.at[s - 4], sf_r.at[s - 4], up)

    pl.loop(8, 12)(lambda s: landed(rb.at[s], sb_r.at[s]))

    def fetch(p):
        x = rb[pl.ds(p * 4, 4)].reshape(256, 256)
        top = x.astype(BF16)
        return x, top, (x - top.astype(F32)).astype(BF16)

    def keep(p, top, rest):
        rows = pl.ds(pl.multiple_of(p * 256, 256), 256)
        xhi[rows, :] = top
        xlo[rows, :] = rest

    def smoothed(p, x, top, rest):
        rows = pl.ds(pl.multiple_of(p * 256, 256), 256)
        beside = jnp.dot(top, adj_ref[...], preferred_element_type=F32)
        beside = beside + jnp.dot(rest, adj_ref[...], preferred_element_type=F32)
        smooth = x * lam_ref[pl.ds(2 * k8 + e, 1), :] + 0.15 * beside
        stop = smooth.astype(BF16)
        shi[rows, :] = stop
        slo[rows, :] = (smooth - stop.astype(F32)).astype(BF16)

    @pl.loop(0, 4)
    def _(p):
        x, top, rest = fetch(p)
        keep(p, top, rest)
        smoothed(p, x, top, rest)

    @pl.loop(0, 2)
    def _(p):
        pl.loop(0, 4)(lambda s: landed(rb.at[16 + p * 4 + s], sf_r.at[p * 4 + s]))
        x, top, rest = fetch(4 + p)
        keep(4 + p, top, rest)

    pl.loop(0, 4)(lambda s: landed(rb.at[24 + s], sf_r.at[8 + s]))
    smoothed(4, *fetch(6))

    def tile(q):
        p, j = q // 4, q % 4
        before = (p == 3) & (j >= 1)
        p, o = jnp.where(before, 4, p), jnp.where(before, j - 1, p + j)
        p = pl.ds(pl.multiple_of(p * 256, 256), 256)
        o = pl.ds(pl.multiple_of(o * 256, 256), 256)
        total = lax.dot_general(shi[p, :], xlo[o, :], NT, preferred_element_type=F32)
        total = total + lax.dot_general(slo[p, :], xhi[o, :], NT, preferred_element_type=F32)
        return total + lax.dot_general(shi[p, :], xhi[o, :], NT, preferred_element_type=F32)

    def turn(n, core):
        return jnp.where(n < 7, (k8 + 1 + (n + 3 * core + 2 * k8) % 7) % 8, k8)

    @pl.loop(0, 8)
    def _(n):
        i = turn(n, 1 - e)
        q = 8 * (1 - e) + i
        part[q] = tile(q)
        send(part.at[q], r1.at[i], s1_s.at[i], s1_r.at[i], other)

    upper, lower = pl.ds(0, 128), pl.ds(128, 128)

    @pl.loop(0, 8)
    def _(n):
        i = turn(n, e)
        q = 8 * e + i
        total = tile(q)
        landed(r1.at[i], s1_r.at[i])
        part[q] = total + r1[i]

        @pl.when(n < 7)
        def _():
            send(part.at[q, upper], r2.at[k8, upper], s2_s.at[i, 0], s2_r.at[k8, 0], mate(i))

    r2[k8] = part[8 * e + k8]

    for h, rows in enumerate((upper, lower)):

        @pl.loop(0, 7)
        def _(n):
            i = (k8 + 1 + n) % 8
            landed(r2.at[i, rows], s2_r.at[i, h])

        if h == 0:

            @pl.loop(0, 7)
            def _(n):
                i = turn(n, e)
                send(part.at[8 * e + i, lower], r2.at[k8, lower], s2_s.at[i, 1], s2_r.at[k8, 1], mate(i))

        total = r2[0, rows]
        for i in range(1, 8):
            total = total + r2[i, rows]
        across[h] = total.T.reshape(4, 64, 128)
        along[h] = total.reshape(2, 64, 256)

        @pl.loop(0, 4)
        def _(i):
            r = (i + pln) % 4
            send(across.at[h, r], o_ref.at[3 + gap, :, rows], sx_s.at[h, r], so_r.at[3 + gap, h], (panel, r))

        @pl.when(gap >= 1)
        def _():
            @pl.loop(0, 2)
            def _(i):
                send(along.at[h, i], o_ref.at[3 - gap], sy_s.at[h, i], so_r.at[3 - gap, 0], (facing, 2 * h + i))

    pl.loop(0, 3)(lambda m: landed(o_ref.at[m], so_r.at[m, 0]))

    @pl.loop(3, 7)
    def _(m):
        landed(o_ref.at[m, :, upper], so_r.at[m, 0])
        landed(o_ref.at[m, :, lower], so_r.at[m, 1])

    pl.loop(0, 16)(lambda k: sent(y_ref.at[k], sa_s.at[k], a_to(k)))
    pl.loop(0, 16)(lambda s: sent(ra.at[s], sb_s.at[s], b_to(s // 2)))
    pl.loop(0, 8)(lambda s: sent(rb.at[s], sf_s.at[s], down))
    pl.loop(0, 4)(lambda s: sent(rb.at[12 + s], sf_s.at[8 + s], up))
    pl.loop(0, 8)(lambda i: sent(part.at[8 * (1 - e) + i], s1_s.at[i], other))

    for h, rows in enumerate((upper, lower)):
        pl.loop(0, 8)(lambda i: sent(part.at[8 * e + i, rows], s2_s.at[i, h], mate(i)))
        pl.loop(0, 4)(lambda r: sent(across.at[h, r], sx_s.at[h, r], (panel, r)))

        @pl.when(gap >= 1)
        def _():
            pl.loop(0, 2)(lambda i: sent(along.at[h, i], sy_s.at[h, i], (facing, 2 * h + i)))


def band_part(jacobian, cell_weight, first, second):
    lane = np.arange(128)
    x, layer = lane % 32, lane // 32
    near = np.abs(x[:, None] - x[None, :]) + np.abs(layer[:, None] - layer[None, :]) == 1
    adjacency = jnp.asarray(np.kron(np.eye(2), near), BF16)
    n = np.arange(32)
    lam = 1 + 0.15 * 2 * np.cos(np.pi * (n + 1) / 33)
    lam = jnp.asarray(np.repeat(lam, 128).reshape(16, 256), F32)
    vmem = pl.BlockSpec(memory_space=pltpu.VMEM)
    dma = pltpu.SemaphoreType.DMA
    counts = ((16,),) * 4 + ((12,),) * 2 + ((8,),) * 2 + ((8, 2),) * 2 + ((2, 4), (2, 2), (7, 2), (6,))
    return pl.pallas_call(
        band_kernel,
        out_shape=jax.ShapeDtypeStruct((7, 64, 256), F32),
        in_specs=[pl.BlockSpec(memory_space=pl.ANY)] * 6,
        out_specs=vmem,
        scratch_shapes=[
            pltpu.VMEM((64, 4096), F32),
            pltpu.VMEM((32, 128), F32),
            pltpu.VMEM((32, 128), jnp.int32),
            pltpu.VMEM((32, 128), jnp.int32),
            pltpu.VMEM((16, 256), F32),
            pltpu.VMEM((256, 256), BF16),
            pltpu.VMEM((16, 64, 256), F32),
            pltpu.VMEM((512, 4096), BF16),
            pltpu.VMEM((512, 4096), BF16),
            pltpu.VMEM((512, 4096), BF16),
            pltpu.VMEM((512, 512), F32),
            pltpu.VMEM((16, 64, 256), F32),
            pltpu.VMEM((28, 64, 256), F32),
            pltpu.VMEM((1536, 256), BF16),
            pltpu.VMEM((1536, 256), BF16),
            pltpu.VMEM((1280, 256), BF16),
            pltpu.VMEM((1280, 256), BF16),
            pltpu.VMEM((16, 256, 256), F32),
            pltpu.VMEM((8, 256, 256), F32),
            pltpu.VMEM((8, 256, 256), F32),
            pltpu.VMEM((2, 4, 64, 128), F32),
            pltpu.VMEM((2, 2, 64, 256), F32),
        ]
        + [dma(c) for c in counts],
        compiler_params=pltpu.CompilerParams(collective_id=0, has_side_effects=True, vmem_limit_bytes=48 * 2**20),
    )(jacobian, cell_weight.reshape(32, 128), first, second, lam, adjacency)


def per_device(jacobian, cell_weight, neighbors):
    first, second = places(neighbors)
    return jnp.swapaxes(band_part(jacobian, cell_weight, first, second), 1, 2)


def solution(mesh):
    return jax.shard_map(
        per_device,
        mesh=mesh,
        in_specs=(P(("blk", "rep"), None), P(), P()),
        out_specs=P(None, "blk", "rep"),
        check_vma=False,
    )
```
